512 devices in a mesh: ctx: 32 (over x, z_lo), nbr: 4 (over z_hi, core), mp: 4 (over y).
Axes of the slice: x: 4, y: 4, z: 16 (z_hi: 2, z_lo: 8; z = z_hi * 8 + z_lo), core: 2. Of those that a mesh axis runs over, the one named last changes fastest.
Arguments:
- self_queries: bfloat16 [32768, 4096], P(('ctx', 'nbr'), 'mp'), may hold values from -6 to 6
- self_keys: bfloat16 [32768, 4096], P(('ctx', 'nbr'), 'mp'), may hold values from -6 to 6
- self_values: bfloat16 [32768, 4096], P(('ctx', 'nbr'), 'mp'), may hold values from -6 to 6
- cross_queries: bfloat16 [32768, 4096], P(('ctx', 'nbr'), 'mp'), may hold values from -6 to 6
- neighbour_keys: bfloat16 [384, 128, 4096], P(('ctx', 'nbr'), None, 'mp'), may hold values from -6 to 6
- neighbour_values: bfloat16 [384, 128, 4096], P(('ctx', 'nbr'), None, 'mp'), may hold values from -6 to 6
- neighbour_table: int32 [512, 2], replicated, may hold values from 0 to 11, as said below
- doc_lengths: int32 [33], replicated, may hold values from 1 to 2048, 32768 in all
Outputs:
- self_out: bfloat16 [32768, 4096], P(('ctx', 'nbr'), 'mp')
- cross_out: bfloat16 [32768, 4096], P(('ctx', 'nbr'), 'mp')
The draws below stay inside these ranges and needn't reach their ends.
Inputs may be any that keep to these rules, and one draw needn't show every extreme that they name: `neighbour_table`: id // 3 is the index along nbr of the device of the stretch's ctx group that holds the encoding, id % 3 its slot there. The 2 ids of a stretch differ. The rows of the stretches of one index of ctx+nbr name exactly 2 distinct encodings held by each device of its ctx group.
All inputs are finite; a program needn't handle non-finite values.
Results may differ from the reference program's by a relative error of at most 0.005.
Values may be sent and summed in bfloat16 or wider, within the bound.
No kernel may reach another device: no remote copies, remote signals or barrier semaphores. Data moves between devices by JAX's collectives and lax.ppermute only.
A program may use at most 64 MiB of HBM per device.

```python
import math
import jax
import jax.numpy as jnp
import numpy as np
from jax import lax

HD = 128
SH = 32
CH = 32
STRETCH = 64
NEIGH = 2
NLEN = 128
TOK_DEV = 256
MOST = 2048
TOKENS = 32768
STRETCHES = 512
DOCS = 33
CAP = 2
NB_DEV = 3
POOL = 384
STRETCHES_GROUP = 16
POOL_GROUP = 12
N_NBR = 4


def drawn_rows(key, count, width):
    return jnp.clip(jax.random.normal(key, (count, width), jnp.float32), -6.0, 6.0)


def draw_self_queries(key, part):
    key = jax.random.fold_in(key, 1)
    values = drawn_rows(key, TOKENS, SH * HD)
    return values.astype(jnp.bfloat16)


def draw_self_keys(key, part):
    key = jax.random.fold_in(key, 2)
    values = drawn_rows(key, TOKENS, SH * HD)
    return values.astype(jnp.bfloat16)


def draw_cross_queries(key, part):
    key = jax.random.fold_in(key, 3)
    values = drawn_rows(key, TOKENS, CH * HD)
    return values.astype(jnp.bfloat16)


def draw_neighbour_keys(key, part):
    key = jax.random.fold_in(key, 4)
    values = drawn_rows(key, POOL * NLEN, CH * HD).reshape(POOL, NLEN, CH * HD)
    return values.astype(jnp.bfloat16)


def draw_neighbour_table(key, part):
    key = jax.random.fold_in(key, 5)
    devices = TOKENS // TOK_DEV
    requests = TOK_DEV // STRETCH * NEIGH
    order_key, offset_key = jax.random.split(key)
    orders = jax.vmap(lambda single: jax.random.permutation(single, requests))(jax.random.split(order_key, devices))
    holder = orders // CAP
    repeat = orders % CAP
    offsets = jax.random.randint(offset_key, (devices, N_NBR), 0, NB_DEV)
    begin = jnp.take_along_axis(offsets, holder, axis=1)
    slots = (begin + repeat) % NB_DEV
    return (holder * NB_DEV + slots).reshape(STRETCHES, NEIGH).astype(jnp.int32)


def level_of(rng, shape, cuts, low, top_value):
    loudness = 1.0
    for axis_at, parts in cuts:
        heights = jax.random.uniform(jax.random.fold_in(jax.random.fold_in(rng, 6), axis_at), (parts,), jnp.float32, low / len(cuts), top_value / len(cuts))
        loudness = loudness * jnp.repeat(jnp.exp(heights), shape[axis_at] // parts).reshape((-1,) + (1,) * (len(shape) - 1 - axis_at))
    return loudness


def profile(count, total, limit, lean):
    portions = [(1 << 20) // math.isqrt(standing ** lean) + 1 for standing in range(2, count + 1)]
    rest, given = total - limit - (count - 1), [1] * (count - 1)
    while rest > 0:
        free = [i for i in range(count - 1) if given[i] < limit]
        pool, budget = sum([portions[i] for i in free]), rest
        for i in free:
            addition = min(limit - given[i], max(1, budget * portions[i] // pool), rest)
            given[i] = given[i] + addition
            rest = rest - addition
    return np.array([limit] + given)


def uneven_parts(own_key, amount, total, bound, lean):
    if amount == 2:
        one = jax.random.randint(own_key, (), max(1, total - bound), min(bound, total - 1) + 1)
        return jnp.stack([one, total - one])
    tallies = jnp.asarray(profile(amount, total, bound, lean), jnp.int32)
    pairs = (amount - 1) // 2
    giver, sink = tallies[1:1 + 2 * pairs:2], tallies[2:2 + 2 * pairs:2]
    margin = jnp.minimum(giver - 1, bound - sink)
    moved = jax.random.randint(jax.random.fold_in(own_key, 1), (pairs,), 0, 1 << 20) % (margin + 1)
    tallies = tallies.at[1:1 + 2 * pairs:2].set(giver - moved).at[2:2 + 2 * pairs:2].set(sink + moved)
    return tallies[jax.random.permutation(jax.random.fold_in(own_key, 2), amount)]


def normal_values(own_key, dims, spread, bound, cuts=(), kind=jnp.bfloat16):
    array = spread * jax.random.normal(own_key, dims, jnp.float32)
    if cuts:
        array = array * level_of(own_key, dims, cuts, -0.22, 0.18)
    return jnp.clip(array, -bound, bound).astype(kind)


def setup_inputs(seed: int = 0) -> dict:
    streams_of = jax.random.split(jax.random.key(seed), 9)
    self_queries = draw_self_queries(jax.random.fold_in(streams_of[8], 71), 0)
    self_keys = draw_self_keys(jax.random.fold_in(streams_of[8], 71), 0)
    self_values = normal_values(streams_of[2], (TOKENS, SH * HD), 1.0, 6.0, ((0, 128), (1, 4)))
    cross_queries = draw_cross_queries(jax.random.fold_in(streams_of[8], 71), 0)
    neighbour_keys = draw_neighbour_keys(jax.random.fold_in(streams_of[8], 71), 0)
    neighbour_values = normal_values(streams_of[5], (POOL, NLEN, CH * HD), 1.0, 6.0, ((0, 128), (2, 4)))
    neighbour_table = draw_neighbour_table(jax.random.fold_in(streams_of[8], 71), 0)
    doc_lengths = uneven_parts(streams_of[7], DOCS, TOKENS, MOST, 2).astype(jnp.int32)
    return {"self_queries": self_queries, "self_keys": self_keys, "self_values": self_values, "cross_queries": cross_queries, "neighbour_keys": neighbour_keys, "neighbour_values": neighbour_values, "neighbour_table": neighbour_table, "doc_lengths": doc_lengths}


def doc_starts(doc_lengths, positions):
    ends = jnp.cumsum(doc_lengths)
    chosen = jnp.where(ends[None, :] <= positions[:, None], doc_lengths[None, :], 0)
    return jnp.sum(chosen, axis=1).astype(jnp.int32)


def softmax_context(scores, visible, values):
    scores = jnp.where(visible, scores, -1e30)
    highest = jnp.max(scores, axis=-1, keepdims=True)
    weights = jnp.where(visible, jnp.exp(scores - highest), 0.0)
    totals = jnp.sum(weights, axis=-1)
    rounded = lax.optimization_barrier(weights.astype(jnp.bfloat16)).astype(jnp.float32)
    summed = jnp.einsum('hqk,khd->qhd', rounded, values.astype(jnp.float32))
    return summed / jnp.transpose(totals)[:, :, None]


def reference(self_queries, self_keys, self_values, cross_queries, neighbour_keys, neighbour_values, neighbour_table, doc_lengths):
    width = self_queries.shape[1]
    scale = HD ** -0.5
    positions = jnp.arange(TOKENS, dtype=jnp.int32)
    starts = doc_starts(doc_lengths, positions)
    padding = jnp.zeros((MOST, width), self_keys.dtype)
    padded_keys = jnp.concatenate([padding, self_keys], axis=0)
    padded_values = jnp.concatenate([padding, self_values], axis=0)

    def self_block(index):
        first = (index * TOK_DEV).astype(jnp.int32)
        queries = lax.dynamic_slice_in_dim(self_queries, first, TOK_DEV, 0).reshape(TOK_DEV, SH, HD)
        keys = lax.dynamic_slice_in_dim(padded_keys, first, MOST + TOK_DEV, 0).reshape(MOST + TOK_DEV, SH, HD)
        values = lax.dynamic_slice_in_dim(padded_values, first, MOST + TOK_DEV, 0).reshape(MOST + TOK_DEV, SH, HD)
        query_pos = first + jnp.arange(TOK_DEV, dtype=jnp.int32)
        key_pos = first - MOST + jnp.arange(MOST + TOK_DEV, dtype=jnp.int32)
        query_start = lax.dynamic_slice_in_dim(starts, first, TOK_DEV, 0)
        visible = (key_pos[None, :] <= query_pos[:, None]) & (key_pos[None, :] >= query_start[:, None])
        scores = jnp.einsum('qhd,khd->hqk', queries.astype(jnp.float32), keys.astype(jnp.float32)) * scale
        context = softmax_context(scores, visible[None], values)
        return context.reshape(TOK_DEV, SH * HD).astype(jnp.bfloat16)

    self_out = lax.map(self_block, jnp.arange(TOKENS // TOK_DEV, dtype=jnp.int32)).reshape(TOKENS, SH * HD)

    def cross_block(stretch):
        group = stretch // STRETCHES_GROUP
        rows = (group * POOL_GROUP + neighbour_table[stretch]).astype(jnp.int32)
        keys = neighbour_keys[rows].reshape(NEIGH * NLEN, CH, HD)
        values = neighbour_values[rows].reshape(NEIGH * NLEN, CH, HD)
        first = (stretch * STRETCH).astype(jnp.int32)
        queries = lax.dynamic_slice_in_dim(cross_queries, first, STRETCH, 0).reshape(STRETCH, CH, HD)
        scores = jnp.einsum('qhd,khd->hqk', queries.astype(jnp.float32), keys.astype(jnp.float32)) * scale
        visible = jnp.ones((1, 1, NEIGH * NLEN), dtype=bool)
        context = softmax_context(scores, visible, values)
        return context.reshape(STRETCH, CH * HD).astype(jnp.bfloat16)

    cross_out = lax.map(cross_block, jnp.arange(STRETCHES, dtype=jnp.int32)).reshape(TOKENS, CH * HD)
    return self_out, cross_out
```

```python
import functools
import jax
import jax.numpy as jnp
from jax import lax
from jax.experimental import pallas as pl
from jax.experimental.pallas import tpu as pltpu
from jax.sharding import PartitionSpec as P

HD = 128
STRETCH = 64
LOG2E = 1.4426950408889634
EXP_SCALE = LOG2E * HD**-0.5
HIDDEN = -1e30
FLOOR = -1e29
ALL = ("ctx", "nbr")


def shift(value, by):
    count = lax.axis_size(ALL)
    return lax.ppermute(value, ALL, [(d, (d + by) % count) for d in range(count)])


def swap(value, bit):
    count = lax.axis_size(ALL)
    return lax.ppermute(value, ALL, [(d, d ^ bit) for d in range(count)])


def self_kernel(blocks, first, last, meta, *refs):
    refs = list(refs)
    q_ref = refs.pop(0)
    start_ref = refs.pop(0)
    keys = [refs.pop(0) for _ in blocks]
    values = [refs.pop(0) for _ in blocks]
    if not first:
        acc_in, top_in, total_in = refs.pop(0), refs.pop(0), refs.pop(0)
    if last:
        out_ref = refs.pop(0)
        acc, top, total = refs
    else:
        acc, top, total = refs
    half = q_ref.shape[0] // 2
    if first:
        acc[...] = jnp.zeros_like(acc)
        top[...] = jnp.full_like(top, FLOOR)
        total[...] = jnp.zeros_like(total)
    else:
        acc[...] = acc_in[...]
        top[...] = top_in[...]
        total[...] = total_in[...]
    for qi in range(2):
        rows = pl.ds(qi * half, half)
        q_base = meta[qi]
        q_first = meta[2 + qi]
        for bi, back in enumerate(blocks):
            for ki in range(2):
                k_base = meta[ki] - back * 2 * half
                seen = (k_base <= q_base + half - 1) & (k_base + half - 1 >= q_first)

                @pl.when(seen)
                def _(rows=rows, bi=bi, ki=ki, k_base=k_base, q_base=q_base):
                    cols = pl.ds(ki * half, half)
                    scores = lax.dot_general(
                        q_ref[rows, :],
                        keys[bi][cols, :],
                        (((1,), (1,)), ((), ())),
                        preferred_element_type=jnp.float32,
                    )
                    k_pos = k_base + lax.broadcasted_iota(jnp.int32, (half, half), 1)
                    q_pos = q_base + lax.broadcasted_iota(jnp.int32, (half, half), 0)
                    begin = start_ref[rows, :]
                    begin = jnp.concatenate([begin] * (half // HD), axis=1)
                    scores = jnp.where((k_pos <= q_pos) & (k_pos >= begin), scores, HIDDEN)
                    old = top[0, rows, :]
                    new = jnp.maximum(old, jnp.max(scores, axis=1, keepdims=True))
                    wide = jnp.concatenate([new] * (half // HD), axis=1)
                    weights = jnp.exp2((scores - wide) * EXP_SCALE)
                    factor = jnp.exp2((old - new) * EXP_SCALE)
                    top[0, rows, :] = new
                    total[0, rows, :] = total[0, rows, :] * factor + jnp.sum(
                        weights, axis=1, keepdims=True
                    )
                    acc[rows, :] = acc[rows, :] * factor + jnp.dot(
                        weights.astype(jnp.bfloat16),
                        values[bi][cols, :],
                        preferred_element_type=jnp.float32,
                    )

    if last:
        out_ref[...] = (acc[...] / total[0]).astype(out_ref.dtype)


def self_part(meta, queries, starts, blocks, keys, values, state, last):
    rows, width = queries.shape
    heads = width // HD
    column = pl.BlockSpec((rows, HD), lambda h: (0, h))
    stat = pl.BlockSpec((1, rows, HD), lambda h: (h, 0, 0))
    first = state is None
    n = len(blocks)
    in_specs = [
        pl.BlockSpec(memory_space=pltpu.SMEM),
        column,
        pl.BlockSpec((rows, HD), lambda h: (0, 0)),
    ] + [column] * (2 * n)
    args = [meta, queries, starts, *keys, *values]
    if not first:
        in_specs += [column, stat, stat]
        args += list(state)
    state_shapes = (
        jax.ShapeDtypeStruct((rows, width), jnp.float32),
        jax.ShapeDtypeStruct((heads, rows, HD), jnp.float32),
        jax.ShapeDtypeStruct((heads, rows, HD), jnp.float32),
    )
    if last:
        out_shape = jax.ShapeDtypeStruct((rows, width), jnp.bfloat16)
        out_specs = column
        scratch = [
            pltpu.VMEM((rows, HD), jnp.float32),
            pltpu.VMEM((1, rows, HD), jnp.float32),
            pltpu.VMEM((1, rows, HD), jnp.float32),
        ]
    else:
        out_shape = state_shapes
        out_specs = (column, stat, stat)
        scratch = []
    return pl.pallas_call(
        functools.partial(self_kernel, tuple(blocks), first, last),
        grid=(heads,),
        in_specs=in_specs,
        out_specs=out_specs,
        out_shape=out_shape,
        scratch_shapes=scratch,
        compiler_params=pltpu.CompilerParams(vmem_limit_bytes=32 * 1024 * 1024),
    )(*args)


def cross_kernel(per, meta, q_ref, k_ref, v_ref, o_ref, stat_ref, column):
    length = k_ref.shape[1]
    requests = 2 * per
    side = lax.broadcasted_iota(jnp.int32, (STRETCH, 2 * length), 1) < length
    lane = lax.broadcasted_iota(jnp.int32, (STRETCH, HD), 1)
    for t in range(per):
        rows = pl.ds(t * STRETCH, STRETCH)
        a, b = meta[2 * t], meta[2 * t + 1]
        have_a, have_b = meta[requests + 2 * t], meta[requests + 2 * t + 1]
        k = jnp.concatenate([k_ref[a], k_ref[b]], axis=0)
        v = jnp.concatenate([v_ref[a], v_ref[b]], axis=0)
        scores = lax.dot_general(
            q_ref[rows, :], k, (((1,), (1,)), ((), ())), preferred_element_type=jnp.float32
        )
        have = jnp.where(side, have_a, have_b)
        scores = jnp.where(have > 0, scores, HIDDEN)
        top = jnp.maximum(jnp.max(scores, axis=1, keepdims=True), FLOOR)
        weights = jnp.exp2((scores - top) * EXP_SCALE)
        total = jnp.sum(weights, axis=1, keepdims=True)
        o_ref[rows, :] = jnp.dot(
            weights.astype(jnp.bfloat16), v, preferred_element_type=jnp.float32
        ).astype(o_ref.dtype)
        column[rows, :] = jnp.where(lane == 0, top, jnp.where(lane == 1, total, 0.0))
    stat_ref[0] = jnp.transpose(column[...])[:8, :]


def cross_part(meta, queries, keys, values, out_type):
    rows, width = queries.shape
    heads = width // HD
    per = rows // STRETCH
    held, length, _ = keys.shape
    column = pl.BlockSpec((rows, HD), lambda h: (0, h))
    pool = pl.BlockSpec((held, length, HD), lambda h: (0, 0, h))
    return pl.pallas_call(
        functools.partial(cross_kernel, per),
        grid=(heads,),
        in_specs=[pl.BlockSpec(memory_space=pltpu.SMEM), column, pool, pool],
        out_specs=(column, pl.BlockSpec((1, 8, rows), lambda h: (h, 0, 0))),
        out_shape=(
            jax.ShapeDtypeStruct((rows, width), out_type),
            jax.ShapeDtypeStruct((heads, 8, rows), jnp.float32),
        ),
        scratch_shapes=[pltpu.VMEM((rows, HD), jnp.float32)],
        compiler_params=pltpu.CompilerParams(vmem_limit_bytes=32 * 1024 * 1024),
    )(meta, queries, keys, values)


def merge_kernel(oa_ref, ob_ref, sa_ref, sb_ref, out_ref):
    rows = oa_ref.shape[0]
    fill = jnp.zeros((HD - 16, rows), jnp.float32)
    stats = jnp.transpose(jnp.concatenate([sa_ref[0], sb_ref[0], fill], axis=0))
    top_a, total_a = stats[:, 0:1], stats[:, 1:2]
    top_b, total_b = stats[:, 8:9], stats[:, 9:10]
    top = jnp.maximum(top_a, top_b)
    part_a = jnp.exp2((top_a - top) * EXP_SCALE)
    part_b = jnp.exp2((top_b - top) * EXP_SCALE)
    total = total_a * part_a + total_b * part_b
    summed = oa_ref[...] * part_a + ob_ref[...].astype(jnp.float32) * part_b
    out_ref[...] = (summed / total).astype(out_ref.dtype)


def merge(oa, ob, sa, sb):
    rows, width = oa.shape
    heads = width // HD
    column = pl.BlockSpec((rows, HD), lambda h: (0, h))
    stat = pl.BlockSpec((1, 8, rows), lambda h: (h, 0, 0))
    return pl.pallas_call(
        merge_kernel,
        grid=(heads,),
        in_specs=[column, column, stat, stat],
        out_specs=column,
        out_shape=jax.ShapeDtypeStruct((rows, width), jnp.bfloat16),
    )(oa, ob, sa, sb)


def shards(
    self_queries,
    self_keys,
    self_values,
    cross_queries,
    neighbour_keys,
    neighbour_values,
    neighbour_table,
    doc_lengths,
):
    tokens, width = self_queries.shape
    part = width // 2
    device = lax.axis_index(ALL)
    core = device % 2
    zhi = (device // 2) % 2
    chip = device // 2

    far_queries = swap(cross_queries, 2)
    keys_beside = swap(neighbour_keys, 1)
    values_beside = swap(neighbour_values, 1)

    def mine(x):
        return lax.dynamic_slice_in_dim(x, core * part, part, 1)

    def other(x):
        return lax.dynamic_slice_in_dim(x, (1 - core) * part, part, 1)

    trio = (self_keys, self_values, self_queries)
    beside = swap(jnp.stack([other(x) for x in trio]), 1)
    k0, v0, q0 = (jnp.concatenate([mine(x), beside[i]], axis=0) for i, x in enumerate(trio))

    k2 = shift(k0, 4)
    v3 = shift(v0, 6)
    v2 = shift(v0, 4)
    k4 = shift(k2, 4)
    v1 = shift(v3, -4)
    v4 = shift(v2, 4)
    k1 = shift(k4, -6)
    k3 = shift(k1, 4)

    base = jnp.stack([chip * 2 * tokens + core * tokens, chip * 2 * tokens + (1 - core) * tokens])
    positions = (base[:, None] + jnp.arange(tokens, dtype=jnp.int32)[None, :]).reshape(-1)
    ends = jnp.cumsum(doc_lengths)
    starts = jnp.sum(jnp.where(ends[None, :] <= positions[:, None], doc_lengths[None, :], 0), axis=1)
    self_meta = jnp.stack([base[0], base[1], starts[0], starts[tokens]]).astype(jnp.int32)
    starts_wide = jnp.broadcast_to(starts[:, None], (2 * tokens, HD)).astype(jnp.int32)

    def pool_meta(owner):
        per = tokens // STRETCH
        ids = lax.dynamic_slice_in_dim(neighbour_table, owner * per, per, 0).reshape(-1)
        holder, slot = ids // neighbour_keys.shape[0], ids % neighbour_keys.shape[0]
        index = jnp.where(holder % 2 == core, slot, slot + neighbour_keys.shape[0])
        return jnp.concatenate([index, (holder // 2 == zhi).astype(jnp.int32)]).astype(jnp.int32)

    pool_keys = jnp.concatenate([neighbour_keys, keys_beside], axis=0)
    pool_values = jnp.concatenate([neighbour_values, values_beside], axis=0)
    far_sum, far_stat = cross_part(
        pool_meta(device ^ 2), far_queries, pool_keys, pool_values, jnp.bfloat16
    )
    back_sum = swap(far_sum, 2)
    back_stat = swap(far_stat, 2)
    near_sum, near_stat = cross_part(
        pool_meta(device), cross_queries, pool_keys, pool_values, jnp.float32
    )

    state = self_part(self_meta, q0, starts_wide, (0, 2), (k0, k2), (v0, v2), None, False)
    state = self_part(self_meta, q0, starts_wide, (4,), (k4,), (v4,), state, False)
    state = self_part(self_meta, q0, starts_wide, (1,), (k1,), (v1,), state, False)
    both = self_part(self_meta, q0, starts_wide, (3,), (k3,), (v3,), state, True)
    returned = swap(both[tokens:], 1)
    kept = both[:tokens]
    self_out = jnp.where(
        core == 0,
        jnp.concatenate([kept, returned], axis=1),
        jnp.concatenate([returned, kept], axis=1),
    )
    cross_out = merge(near_sum, back_sum, near_stat, back_stat)
    return self_out, cross_out


def solution(mesh):
    rows = P(("ctx", "nbr"), "mp")
    pool = P(("ctx", "nbr"), None, "mp")
    return jax.shard_map(
        shards,
        mesh=mesh,
        in_specs=(rows, rows, rows, rows, pool, pool, P(), P()),
        out_specs=(rows, rows),
        check_vma=False,
    )
```

```python
import functools
import jax
import jax.numpy as jnp
from jax import lax
from jax.experimental import pallas as pl
from jax.experimental.pallas import tpu as pltpu
from jax.sharding import PartitionSpec as P

HD = 128
STRETCH = 64
LOG2E = 1.4426950408889634
EXP_SCALE = LOG2E * HD**-0.5
HIDDEN = -1e30
FLOOR = -1e29
ALL = ("ctx", "nbr")
RUN = 8
SMALL = pl.CostEstimate(flops=1, bytes_accessed=1, transcendentals=0)
LARGE = pl.CostEstimate(flops=10**11, bytes_accessed=10**8, transcendentals=0)


def place(d):
    return d // 4 % RUN, d // 2 % 2


def shift(value, by, to=lambda low, high: True):
    count = lax.axis_size(ALL)
    pairs = [(d, (d + by) % count) for d in range(count)]
    return lax.ppermute(value, ALL, [(a, b) for a, b in pairs if to(*place(b))])


def swap(value, bit):
    count = lax.axis_size(ALL)
    return lax.ppermute(value, ALL, [(d, d ^ bit) for d in range(count)])


def around(value, by):
    count = lax.axis_size(ALL)

    def target(d):
        low, high = place(d)
        z = (high * RUN + low + by) % (2 * RUN)
        return d + (z % RUN - low) * 4 + (z // RUN - high) * 2

    return lax.ppermute(value, ALL, [(d, target(d)) for d in range(count)])


def held_back(value, after):
    hbm = pl.BlockSpec(memory_space=pl.ANY)
    return pl.pallas_call(
        lambda *refs: None,
        in_specs=[hbm] * (1 + len(after)),
        out_specs=hbm,
        out_shape=jax.ShapeDtypeStruct(value.shape, value.dtype),
        input_output_aliases={0: 0},
        cost_estimate=SMALL,
    )(value, *after)


def self_kernel(blocks, first, last, skip, meta, *refs):
    refs = list(refs)
    q_ref = refs.pop(0)
    start_ref = refs.pop(0)
    pairs = [refs.pop(0) for _ in blocks]
    if not first:
        acc_in, top_in, total_in = refs.pop(0), refs.pop(0), refs.pop(0)
    refs = refs[skip:]
    if last:
        kept_ref, sent_ref = refs.pop(0), refs.pop(0)
    acc, top, total = refs
    rows = q_ref.shape[0]
    half = rows // 2
    if first:
        acc[...] = jnp.zeros_like(acc)
        top[...] = jnp.full_like(top, FLOOR)
        total[...] = jnp.zeros_like(total)
    else:
        acc[...] = acc_in[...]
        top[...] = top_in[...]
        total[...] = total_in[...]
    for bi, (back, flag) in enumerate(blocks):
        away = back * rows
        chip_first = jnp.minimum(meta[0], meta[1])
        seen = (chip_first - away + rows - 1 >= meta[2]) & (chip_first >= away)
        if flag:
            seen &= meta[2 + flag] > 0
        for qi in range(2):

            @pl.when(seen)
            def _(qi=qi, bi=bi, away=away):
                mine = pl.ds(qi * half, half)
                scores = lax.dot_general(
                    q_ref[mine, :],
                    pairs[bi][0],
                    (((1,), (1,)), ((), ())),
                    preferred_element_type=jnp.float32,
                )
                spot = lax.broadcasted_iota(jnp.int32, (half, half), 1)
                k_pos = jnp.concatenate([spot + meta[0], spot + meta[1]], axis=1) - away
                q_pos = meta[qi] + lax.broadcasted_iota(jnp.int32, (half, rows), 0)
                begin = jnp.concatenate([start_ref[mine, :]] * (rows // HD), axis=1)
                scores = jnp.where((k_pos <= q_pos) & (k_pos >= begin), scores, HIDDEN)
                old = top[0, mine, :]
                new = jnp.maximum(old, jnp.max(scores, axis=1, keepdims=True))
                wide = jnp.concatenate([new] * (rows // HD), axis=1)
                weights = jnp.exp2((scores - wide) * EXP_SCALE)
                factor = jnp.exp2((old - new) * EXP_SCALE)
                top[0, mine, :] = new
                total[0, mine, :] = total[0, mine, :] * factor + jnp.sum(
                    weights, axis=1, keepdims=True
                )
                acc[mine, :] = acc[mine, :] * factor + jnp.dot(
                    weights.astype(jnp.bfloat16), pairs[bi][1], preferred_element_type=jnp.float32
                )

    if last:
        out = (acc[...] / total[0]).astype(kept_ref.dtype)
        kept_ref[...] = out[:half]
        sent_ref[...] = out[half:]


def self_part(meta, queries, starts, blocks, pairs, state, last, after, cost):
    rows, width = queries.shape
    heads = width // HD
    column = pl.BlockSpec((rows, HD), lambda h: (0, h))
    pair = pl.BlockSpec((2, rows, HD), lambda h: (0, 0, h))
    stat = pl.BlockSpec((1, rows, HD), lambda h: (h, 0, 0))
    first = state is None
    in_specs = [
        pl.BlockSpec(memory_space=pltpu.SMEM),
        column,
        pl.BlockSpec((rows, HD), lambda h: (0, 0)),
    ] + [pair] * len(blocks)
    args = [meta, queries, starts, *pairs]
    if not first:
        in_specs += [column, stat, stat]
        args += list(state)
    in_specs += [pl.BlockSpec(memory_space=pl.ANY)] * len(after)
    args += list(after)
    if last:
        out_shape = (jax.ShapeDtypeStruct((rows // 2, width), jnp.bfloat16),) * 2
        out_specs = (pl.BlockSpec((rows // 2, HD), lambda h: (0, h)),) * 2
        scratch = [
            pltpu.VMEM((rows, HD), jnp.float32),
            pltpu.VMEM((1, rows, HD), jnp.float32),
            pltpu.VMEM((1, rows, HD), jnp.float32),
        ]
    else:
        out_shape = (
            jax.ShapeDtypeStruct((rows, width), jnp.float32),
            jax.ShapeDtypeStruct((heads, rows, HD), jnp.float32),
            jax.ShapeDtypeStruct((heads, rows, HD), jnp.float32),
        )
        out_specs = (column, stat, stat)
        scratch = []
    return pl.pallas_call(
        functools.partial(self_kernel, tuple(blocks), first, last, len(after)),
        grid=(heads,),
        in_specs=in_specs,
        out_specs=out_specs,
        out_shape=out_shape,
        scratch_shapes=scratch,
        compiler_params=pltpu.CompilerParams(vmem_limit_bytes=32 * 1024 * 1024),
        cost_estimate=cost,
    )(*args)


def cross_kernel(per, travels, meta, q_ref, k_here, v_here, side, *refs):
    if travels:
        o_ref, column = refs[-2:]
    else:
        o_ref, stat_ref, column = refs[-3:]
    k_side, v_side = side.at[0], side.at[1]
    length = k_here.shape[1]
    rows, width = q_ref.shape
    heads = width // HD
    requests = 2 * per

    def pick(here, side, r, cols):
        slot, beside = meta[r], meta[requests + r]
        return jnp.where(beside > 0, side[slot, :, cols], here[slot, :, cols])

    shape = (STRETCH, 2 * length)
    first = lax.broadcasted_iota(jnp.int32, shape, 1) < length
    have = jnp.concatenate(
        [
            jnp.where(first, meta[2 * requests + 2 * t], meta[2 * requests + 2 * t + 1])
            for t in range(per)
        ],
        axis=0,
    )
    lane = lax.broadcasted_iota(jnp.int32, (rows, HD), 1)
    stats = jnp.zeros((rows, HD), jnp.float32)
    for h in range(heads):
        cols = slice(h * HD, (h + 1) * HD)
        scores = []
        for t in range(per):
            keys = jnp.concatenate([pick(k_here, k_side, 2 * t + j, cols) for j in range(2)], axis=0)
            scores.append(
                lax.dot_general(
                    q_ref[t * STRETCH : (t + 1) * STRETCH, cols],
                    keys,
                    (((1,), (1,)), ((), ())),
                    preferred_element_type=jnp.float32,
                )
            )
        scores = jnp.where(have > 0, jnp.concatenate(scores, axis=0), HIDDEN)
        top = jnp.maximum(jnp.max(scores, axis=1, keepdims=True), FLOOR)
        weights = jnp.exp2((scores - top) * EXP_SCALE)
        total = jnp.sum(weights, axis=1, keepdims=True)
        weights = weights.astype(jnp.bfloat16)
        stats = jnp.where(lane == h, top, jnp.where(lane == heads + h, total, stats))
        for t in range(per):
            values = jnp.concatenate([pick(v_here, v_side, 2 * t + j, cols) for j in range(2)], axis=0)
            o_ref[t * STRETCH : (t + 1) * STRETCH, cols] = jnp.dot(
                weights[t * STRETCH : (t + 1) * STRETCH],
                values,
                preferred_element_type=jnp.float32,
            ).astype(o_ref.dtype)
    column[...] = stats
    stats = jnp.transpose(column[...])[: 2 * heads, :]
    if travels:
        for i in range(3):
            piece = stats.astype(jnp.bfloat16)
            o_ref[rows : rows + 2 * heads, i * rows : (i + 1) * rows] = piece
            stats = stats - piece.astype(jnp.float32)
        o_ref[rows : rows + 2 * heads, 3 * rows :] = jnp.zeros(
            (2 * heads, width - 3 * rows), jnp.bfloat16
        )
    else:
        stat_ref[...] = stats


def cross_part(meta, queries, pool, travels, after, cost):
    rows, width = queries.shape
    heads = width // HD
    vmem = pl.BlockSpec(memory_space=pltpu.VMEM)
    if travels:
        out_specs = vmem
        out_shape = jax.ShapeDtypeStruct((rows + 2 * heads, width), jnp.bfloat16)
    else:
        out_specs = (vmem, vmem)
        out_shape = (
            jax.ShapeDtypeStruct((rows, width), jnp.float32),
            jax.ShapeDtypeStruct((2 * heads, rows), jnp.float32),
        )
    return pl.pallas_call(
        functools.partial(cross_kernel, rows // STRETCH, travels),
        in_specs=[pl.BlockSpec(memory_space=pltpu.SMEM)]
        + [vmem] * 4
        + [pl.BlockSpec(memory_space=pl.ANY)] * len(after),
        out_specs=out_specs,
        out_shape=out_shape,
        scratch_shapes=[pltpu.VMEM((rows, HD), jnp.float32)],
        compiler_params=pltpu.CompilerParams(vmem_limit_bytes=32 * 1024 * 1024),
        cost_estimate=cost,
    )(meta, queries, *pool, *after)


def merge_kernel(oa_ref, ob_ref, sa_ref, out_ref):
    rows, width = oa_ref.shape
    heads = width // HD
    pieces = ob_ref[rows : rows + 2 * heads, : 3 * rows].astype(jnp.float32)
    far = pieces[:, :rows] + pieces[:, rows : 2 * rows] + pieces[:, 2 * rows :]
    fill = jnp.zeros((HD - 4 * heads, rows), jnp.float32)
    stats = jnp.transpose(jnp.concatenate([sa_ref[...], far, fill], axis=0))
    for h in range(heads):
        cols = slice(h * HD, (h + 1) * HD)
        top_a, total_a, top_b, total_b = (
            stats[:, i * heads + h : i * heads + h + 1] for i in range(4)
        )
        top = jnp.maximum(top_a, top_b)
        part_a = jnp.exp2((top_a - top) * EXP_SCALE)
        part_b = jnp.exp2((top_b - top) * EXP_SCALE)
        share = 1.0 / (total_a * part_a + total_b * part_b)
        out_ref[:, cols] = (
            oa_ref[:, cols] * (part_a * share)
            + ob_ref[:rows, cols].astype(jnp.float32) * (part_b * share)
        ).astype(out_ref.dtype)


def merge(oa, ob, sa):
    rows, width = oa.shape
    vmem = pl.BlockSpec(memory_space=pltpu.VMEM)
    return pl.pallas_call(
        merge_kernel,
        in_specs=[vmem] * 3,
        out_specs=vmem,
        out_shape=jax.ShapeDtypeStruct((rows, width), jnp.bfloat16),
        compiler_params=pltpu.CompilerParams(vmem_limit_bytes=32 * 1024 * 1024),
        cost_estimate=SMALL,
    )(oa, ob, sa)


def shards(
    self_queries,
    self_keys,
    self_values,
    cross_queries,
    neighbour_keys,
    neighbour_values,
    neighbour_table,
    doc_lengths,
):
    tokens, width = self_queries.shape
    part = width // 2
    device = lax.axis_index(ALL)
    core = device % 2
    zhi = (device // 2) % 2
    chip = device // 2

    far_queries = swap(cross_queries, 2)

    def mine(x):
        return lax.dynamic_slice_in_dim(x, core * part, part, 1)

    def other(x):
        return lax.dynamic_slice_in_dim(x, (1 - core) * part, part, 1)

    trio = (self_keys, self_values, self_queries)
    beside = swap(jnp.stack([other(x) for x in trio]), 1)
    kv0 = jnp.stack([jnp.concatenate([mine(x), beside[i]]) for i, x in enumerate(trio[:2])])
    q0 = jnp.concatenate([mine(self_queries), beside[2]])
    pool = held_back(jnp.stack([neighbour_keys, neighbour_values]), (kv0,))
    pool_beside = swap(pool, 1)

    base = jnp.stack([chip * 2 * tokens + core * tokens, chip * 2 * tokens + (1 - core) * tokens])
    positions = (base[:, None] + jnp.arange(tokens, dtype=jnp.int32)[None, :]).reshape(-1)
    ends = jnp.cumsum(doc_lengths)
    starts = jnp.sum(jnp.where(ends[None, :] <= positions[:, None], doc_lengths[None, :], 0), axis=1)
    low, high = place(device)
    flags = [low > 0, low == 0, low < RUN - 1, low == RUN - 1]
    self_meta = jnp.stack(
        [base[0], base[1], jnp.minimum(starts[0], starts[tokens]), *flags], dtype=jnp.int32
    )
    starts_wide = jnp.broadcast_to(starts[:, None], (2 * tokens, HD)).astype(jnp.int32)

    def attend(blocks, pairs, state, last=False, after=(), cost=SMALL):
        return self_part(
            self_meta, q0, starts_wide, blocks, pairs, state, last, after, cost
        )

    kv3 = shift(kv0, 6)
    kv2 = shift(kv0, 4)
    kv4_far = shift(kv0, 8, lambda low, high: low == 0)

    state = attend(((0, 0),), (kv0,), None, cost=LARGE)
    def pool_meta(owner):
        per = tokens // STRETCH
        ids = lax.dynamic_slice_in_dim(neighbour_table, owner * per, per, 0).reshape(-1)
        holder, slot = ids // neighbour_keys.shape[0], ids % neighbour_keys.shape[0]
        return jnp.concatenate([slot, holder % 2 != core, holder // 2 == zhi]).astype(jnp.int32)

    pool = (neighbour_keys, neighbour_values, pool_beside)
    near_sum, near_stat = cross_part(
        pool_meta(device), cross_queries, pool, False, state[:1], SMALL
    )
    far_sum = cross_part(
        pool_meta(device ^ 2), far_queries, pool, True, (near_stat,), SMALL
    )
    nearly = around(far_sum, 7)
    kv2 = held_back(kv2, (nearly,))
    kv4 = shift(kv2, 4, lambda low, high: low > 0)
    kv1_edge = lax.ppermute(
        jnp.where(high == 0, kv2, kv4_far),
        ALL,
        [
            (d, (d - 2 - 4 * place(d)[1]) % lax.axis_size(ALL))
            for d in range(lax.axis_size(ALL))
            if place(d)[0] == 0
        ],
    )
    state = attend(
        ((2, 0), (4, 1), (4, 2)),
        (kv2, kv4, kv4_far),
        state,
        after=(far_sum,),
    )
    kv3 = held_back(kv3, (kv2,))
    kv1 = shift(kv3, -4, lambda low, high: low < RUN - 1)
    back_sum = around(nearly, 1)
    state = attend(((3, 0),), (kv3,), state)
    kept, sent = attend(((1, 3), (1, 4)), (kv1, kv1_edge), state, True)
    returned = swap(sent, 1)
    self_out = jnp.where(
        core == 0,
        jnp.concatenate([kept, returned], axis=1),
        jnp.concatenate([returned, kept], axis=1),
    )
    cross_out = merge(near_sum, back_sum, near_stat)
    return self_out, cross_out


def solution(mesh):
    rows = P(("ctx", "nbr"), "mp")
    pool = P(("ctx", "nbr"), None, "mp")
    return jax.shard_map(
        shards,
        mesh=mesh,
        in_specs=(rows, rows, rows, rows, pool, pool, P(), P()),
        out_specs=(rows, rows),
        check_vma=False,
    )
```

```python
import functools
import jax
import jax.numpy as jnp
from jax import lax
from jax.experimental import pallas as pl
from jax.experimental.pallas import tpu as pltpu
from jax.sharding import PartitionSpec as P

HD = 128
STRETCH = 64
LOG2E = 1.4426950408889634
EXP_SCALE = LOG2E * HD**-0.5
HIDDEN = -1e30
FLOOR = -1e29
ALL = ("ctx", "nbr")
RUN = 8
MEDIUM = pl.CostEstimate(flops=1, bytes_accessed=10**7, transcendentals=0)
SMALL = pl.CostEstimate(flops=1, bytes_accessed=1, transcendentals=0)
LARGE = pl.CostEstimate(flops=10**11, bytes_accessed=10**8, transcendentals=0)


def place(d):
    return d // 4 % RUN, d // 2 % 2


def shift(value, by, to=lambda low, high: True):
    count = lax.axis_size(ALL)
    pairs = [(d, (d + by) % count) for d in range(count)]
    return lax.ppermute(value, ALL, [(a, b) for a, b in pairs if to(*place(b))])


def route(value, by):
    count = lax.axis_size(ALL)
    steps = [(d, by(*place(d))) for d in range(count)]
    return lax.ppermute(value, ALL, [(d, (d + n) % count) for d, n in steps if n is not None])


def swap(value, bit):
    count = lax.axis_size(ALL)
    return lax.ppermute(value, ALL, [(d, d ^ bit) for d in range(count)])


def around(value, by):
    count = lax.axis_size(ALL)

    def target(d):
        low, high = place(d)
        z = (high * RUN + low + by) % (2 * RUN)
        return d + (z % RUN - low) * 4 + (z // RUN - high) * 2

    return lax.ppermute(value, ALL, [(d, target(d)) for d in range(count)])


def held_back(value, after):
    hbm = pl.BlockSpec(memory_space=pl.ANY)
    return pl.pallas_call(
        lambda *refs: None,
        in_specs=[hbm] * (1 + len(after)),
        out_specs=hbm,
        out_shape=jax.ShapeDtypeStruct(value.shape, value.dtype),
        input_output_aliases={0: 0},
        cost_estimate=SMALL,
    )(value, *after)


def self_kernel(blocks, first, last, skip, meta, *refs):
    refs = list(refs)
    q_ref = refs.pop(0)
    start_ref = refs.pop(0)
    keys = [refs.pop(0) for _ in blocks]
    values = [refs.pop(0) for _ in blocks]
    if not first:
        acc_in, top_in, total_in = refs.pop(0), refs.pop(0), refs.pop(0)
    refs = refs[skip:]
    if last:
        kept_ref, sent_ref = refs.pop(0), refs.pop(0)
    acc, top, total = refs
    rows = q_ref.shape[0]
    half = rows // 2
    if first:
        acc[...] = jnp.zeros_like(acc)
        top[...] = jnp.full_like(top, FLOOR)
        total[...] = jnp.zeros_like(total)
    else:
        acc[...] = acc_in[...]
        top[...] = top_in[...]
        total[...] = total_in[...]
    for bi, (back, flag) in enumerate(blocks):
        away = back * rows
        chip_first = jnp.minimum(meta[0], meta[1])
        seen = (chip_first - away + rows - 1 >= meta[2]) & (chip_first >= away)
        if flag:
            seen &= meta[2 + flag] > 0
        for qi in range(2):

            @pl.when(seen)
            def _(qi=qi, bi=bi, away=away):
                mine = pl.ds(qi * half, half)
                scores = lax.dot_general(
                    q_ref[mine, :],
                    keys[bi][...],
                    (((1,), (1,)), ((), ())),
                    preferred_element_type=jnp.float32,
                )
                spot = lax.broadcasted_iota(jnp.int32, (half, half), 1)
                k_pos = jnp.concatenate([spot + meta[0], spot + meta[1]], axis=1) - away
                q_pos = meta[qi] + lax.broadcasted_iota(jnp.int32, (half, rows), 0)
                begin = jnp.concatenate([start_ref[mine, :]] * (rows // HD), axis=1)
                scores = jnp.where((k_pos <= q_pos) & (k_pos >= begin), scores, HIDDEN)
                old = top[0, mine, :]
                new = jnp.maximum(old, jnp.max(scores, axis=1, keepdims=True))
                wide = jnp.concatenate([new] * (rows // HD), axis=1)
                weights = jnp.exp2((scores - wide) * EXP_SCALE)
                factor = jnp.exp2((old - new) * EXP_SCALE)
                top[0, mine, :] = new
                total[0, mine, :] = total[0, mine, :] * factor + jnp.sum(
                    weights, axis=1, keepdims=True
                )
                acc[mine, :] = acc[mine, :] * factor + jnp.dot(
                    weights.astype(jnp.bfloat16), values[bi][...], preferred_element_type=jnp.float32
                )

    if last:
        out = (acc[...] / total[0]).astype(kept_ref.dtype)
        kept_ref[...] = out[:half]
        sent_ref[...] = out[half:]


def self_part(meta, queries, starts, blocks, pairs, state, last, after, cost):
    rows, width = queries.shape
    heads = width // HD
    column = pl.BlockSpec((rows, HD), lambda h: (0, h))
    layer = [pl.BlockSpec((None, rows, HD), lambda h, i=i: (i, 0, h)) for i in range(2)]
    stat = pl.BlockSpec((1, rows, HD), lambda h: (h, 0, 0))
    first = state is None
    operands = [k for k, _ in pairs] + [v for _, v in pairs]
    in_specs = [
        pl.BlockSpec(memory_space=pltpu.SMEM),
        column,
        pl.BlockSpec((rows, HD), lambda h: (0, 0)),
    ] + [column if at is None else layer[at] for _, at in operands]
    args = [meta, queries, starts] + [x for x, _ in operands]
    if not first:
        in_specs += [column, stat, stat]
        args += list(state)
    in_specs += [pl.BlockSpec(memory_space=pl.ANY)] * len(after)
    args += list(after)
    if last:
        out_shape = (jax.ShapeDtypeStruct((rows // 2, width), jnp.bfloat16),) * 2
        out_specs = (pl.BlockSpec((rows // 2, HD), lambda h: (0, h)),) * 2
        scratch = [
            pltpu.VMEM((rows, HD), jnp.float32),
            pltpu.VMEM((1, rows, HD), jnp.float32),
            pltpu.VMEM((1, rows, HD), jnp.float32),
        ]
    else:
        out_shape = (
            jax.ShapeDtypeStruct((rows, width), jnp.float32),
            jax.ShapeDtypeStruct((heads, rows, HD), jnp.float32),
            jax.ShapeDtypeStruct((heads, rows, HD), jnp.float32),
        )
        out_specs = (column, stat, stat)
        scratch = []
    return pl.pallas_call(
        functools.partial(self_kernel, tuple(blocks), first, last, len(after)),
        grid=(heads,),
        in_specs=in_specs,
        out_specs=out_specs,
        out_shape=out_shape,
        scratch_shapes=scratch,
        compiler_params=pltpu.CompilerParams(vmem_limit_bytes=32 * 1024 * 1024),
        cost_estimate=cost,
    )(*args)


def cross_kernel(per, travels, meta, q_ref, k_here, v_here, side, *refs):
    if travels:
        o_ref, column = refs[-2:]
    else:
        o_ref, stat_ref, column = refs[-3:]
    k_side, v_side = side.at[0], side.at[1]
    length = k_here.shape[1]
    rows, width = q_ref.shape
    heads = width // HD
    requests = 2 * per

    def pick(here, side, r, cols):
        slot, beside = meta[r], meta[requests + r]
        return jnp.where(beside > 0, side[slot, :, cols], here[slot, :, cols])

    shape = (STRETCH, 2 * length)
    first = lax.broadcasted_iota(jnp.int32, shape, 1) < length
    have = jnp.concatenate(
        [
            jnp.where(first, meta[2 * requests + 2 * t], meta[2 * requests + 2 * t + 1])
            for t in range(per)
        ],
        axis=0,
    )
    lane = lax.broadcasted_iota(jnp.int32, (rows, HD), 1)
    stats = jnp.zeros((rows, HD), jnp.float32)
    for h in range(heads):
        cols = slice(h * HD, (h + 1) * HD)
        scores = []
        for t in range(per):
            keys = jnp.concatenate([pick(k_here, k_side, 2 * t + j, cols) for j in range(2)], axis=0)
            scores.append(
                lax.dot_general(
                    q_ref[t * STRETCH : (t + 1) * STRETCH, cols],
                    keys,
                    (((1,), (1,)), ((), ())),
                    preferred_element_type=jnp.float32,
                )
            )
        scores = jnp.where(have > 0, jnp.concatenate(scores, axis=0), HIDDEN)
        top = jnp.maximum(jnp.max(scores, axis=1, keepdims=True), FLOOR)
        weights = jnp.exp2((scores - top) * EXP_SCALE)
        total = jnp.sum(weights, axis=1, keepdims=True)
        weights = weights.astype(jnp.bfloat16)
        stats = jnp.where(lane == h, top, jnp.where(lane == heads + h, total, stats))
        for t in range(per):
            values = jnp.concatenate([pick(v_here, v_side, 2 * t + j, cols) for j in range(2)], axis=0)
            o_ref[t * STRETCH : (t + 1) * STRETCH, cols] = jnp.dot(
                weights[t * STRETCH : (t + 1) * STRETCH],
                values,
                preferred_element_type=jnp.float32,
            ).astype(o_ref.dtype)
    column[...] = stats
    stats = jnp.transpose(column[...])[: 2 * heads, :]
    if travels:
        for i in range(3):
            piece = stats.astype(jnp.bfloat16)
            o_ref[rows : rows + 2 * heads, i * rows : (i + 1) * rows] = piece
            stats = stats - piece.astype(jnp.float32)
        o_ref[rows : rows + 2 * heads, 3 * rows :] = jnp.zeros(
            (2 * heads, width - 3 * rows), jnp.bfloat16
        )
    else:
        stat_ref[...] = stats


def cross_part(meta, queries, pool, travels, after, cost):
    rows, width = queries.shape
    heads = width // HD
    vmem = pl.BlockSpec(memory_space=pltpu.VMEM)
    if travels:
        out_specs = vmem
        out_shape = jax.ShapeDtypeStruct((rows + 2 * heads, width), jnp.bfloat16)
    else:
        out_specs = (vmem, vmem)
        out_shape = (
            jax.ShapeDtypeStruct((rows, width), jnp.float32),
            jax.ShapeDtypeStruct((2 * heads, rows), jnp.float32),
        )
    return pl.pallas_call(
        functools.partial(cross_kernel, rows // STRETCH, travels),
        in_specs=[pl.BlockSpec(memory_space=pltpu.SMEM)]
        + [vmem] * 4
        + [pl.BlockSpec(memory_space=pl.ANY)] * len(after),
        out_specs=out_specs,
        out_shape=out_shape,
        scratch_shapes=[pltpu.VMEM((rows, HD), jnp.float32)],
        compiler_params=pltpu.CompilerParams(vmem_limit_bytes=32 * 1024 * 1024),
        cost_estimate=cost,
    )(meta, queries, *pool, *after)


def merge_kernel(oa_ref, ob_ref, sa_ref, *refs):
    out_ref = refs[-1]
    rows, width = oa_ref.shape
    heads = width // HD
    pieces = ob_ref[rows : rows + 2 * heads, : 3 * rows].astype(jnp.float32)
    far = pieces[:, :rows] + pieces[:, rows : 2 * rows] + pieces[:, 2 * rows :]
    fill = jnp.zeros((HD - 4 * heads, rows), jnp.float32)
    stats = jnp.transpose(jnp.concatenate([sa_ref[...], far, fill], axis=0))
    for h in range(heads):
        cols = slice(h * HD, (h + 1) * HD)
        top_a, total_a, top_b, total_b = (
            stats[:, i * heads + h : i * heads + h + 1] for i in range(4)
        )
        top = jnp.maximum(top_a, top_b)
        part_a = jnp.exp2((top_a - top) * EXP_SCALE)
        part_b = jnp.exp2((top_b - top) * EXP_SCALE)
        share = 1.0 / (total_a * part_a + total_b * part_b)
        out_ref[:, cols] = (
            oa_ref[:, cols] * (part_a * share)
            + ob_ref[:rows, cols].astype(jnp.float32) * (part_b * share)
        ).astype(out_ref.dtype)


def merge(oa, ob, sa, after):
    rows, width = oa.shape
    vmem = pl.BlockSpec(memory_space=pltpu.VMEM)
    return pl.pallas_call(
        merge_kernel,
        in_specs=[vmem] * 3 + [pl.BlockSpec(memory_space=pl.ANY)] * len(after),
        out_specs=vmem,
        out_shape=jax.ShapeDtypeStruct((rows, width), jnp.bfloat16),
        compiler_params=pltpu.CompilerParams(vmem_limit_bytes=32 * 1024 * 1024),
        cost_estimate=SMALL,
    )(oa, ob, sa, *after)


def shards(
    self_queries,
    self_keys,
    self_values,
    cross_queries,
    neighbour_keys,
    neighbour_values,
    neighbour_table,
    doc_lengths,
):
    tokens, width = self_queries.shape
    part = width // 2
    device = lax.axis_index(ALL)
    core = device % 2
    zhi = (device // 2) % 2
    chip = device // 2

    near_by = around(cross_queries, 1)

    def mine(x):
        return lax.dynamic_slice_in_dim(x, core * part, part, 1)

    def other(x):
        return lax.dynamic_slice_in_dim(x, (1 - core) * part, part, 1)

    trio = (self_keys, self_values, self_queries)
    beside = swap(jnp.stack([other(x) for x in trio]), 1)
    k0, v0, q0 = (jnp.concatenate([mine(x), beside[i]]) for i, x in enumerate(trio))
    pool_beside = swap(jnp.stack([neighbour_keys, neighbour_values]), 1)
    kv0 = held_back(jnp.stack([k0, v0]), (pool_beside,))

    base = jnp.stack([chip * 2 * tokens + core * tokens, chip * 2 * tokens + (1 - core) * tokens])
    positions = (base[:, None] + jnp.arange(tokens, dtype=jnp.int32)[None, :]).reshape(-1)
    ends = jnp.cumsum(doc_lengths)
    starts = jnp.sum(jnp.where(ends[None, :] <= positions[:, None], doc_lengths[None, :], 0), axis=1)
    low, high = place(device)
    top = RUN - 1
    flags = [
        low > 0,
        low == 0,
        high == 0,
        (high == 0) & (low < top),
        (high == 1) & (low < top),
        low == top,
        (high == 1) & (low > 0),
        (high == 1) & (low == 0),
    ]
    self_meta = jnp.stack(
        [base[0], base[1], jnp.minimum(starts[0], starts[tokens]), *flags], dtype=jnp.int32
    )
    starts_wide = jnp.broadcast_to(starts[:, None], (2 * tokens, HD)).astype(jnp.int32)

    def attend(blocks, pairs, state, last=False, after=(), cost=SMALL):
        return self_part(self_meta, q0, starts_wide, blocks, pairs, state, last, after, cost)

    def both(x):
        return (x, 0), (x, 1)

    k3 = shift(k0, 6)
    v13 = route(
        v0,
        lambda low, high: None if (low, high) == (top, 0) else 2 if high == 0 else 6,
    )
    kv2 = shift(kv0, 4)
    kv4_far = shift(kv0, 8, lambda low, high: low == 0)

    state = attend(((0, 0),), (both(kv0),), None, cost=LARGE)
    far_queries = around(held_back(near_by, state[:1]), 7)
    k3, v13 = (held_back(x, state[:1]) for x in (k3, v13))

    def pool_meta(owner):
        per = tokens // STRETCH
        ids = lax.dynamic_slice_in_dim(neighbour_table, owner * per, per, 0).reshape(-1)
        holder, slot = ids // neighbour_keys.shape[0], ids % neighbour_keys.shape[0]
        return jnp.concatenate([slot, holder % 2 != core, holder // 2 == zhi]).astype(jnp.int32)

    pool = (neighbour_keys, neighbour_values, pool_beside)
    near_sum, near_stat = cross_part(
        pool_meta(device), cross_queries, pool, False, (state[0], k3, v13), MEDIUM
    )
    far_sum = cross_part(pool_meta(device ^ 2), far_queries, pool, True, (near_stat,), SMALL)
    back_sum = swap(far_sum, 2)

    kv2 = held_back(kv2, (far_sum,))
    kv4 = shift(kv2, 4, lambda low, high: low > 0)
    edge = route(
        jnp.where(low == top, kv0, jnp.where(high == 0, kv2, kv4_far)),
        lambda low, high: 6 if (low, high) == (top, 0) else None if low else -2 - 4 * high,
    )
    k1 = shift(k3, -4, lambda low, high: low < top)
    v31 = route(
        v13,
        lambda low, high: (4 if low < top else None) if high else (-4 if low > 0 else None),
    )
    state = attend(
        ((2, 0), (4, 1), (4, 2)),
        (both(kv2), both(kv4), both(kv4_far)),
        state,
    )
    state = attend(((3, 3),), (((k3, None), (v13, None)),), state)
    cross_out = merge(near_sum, back_sum, near_stat, ())
    kept, sent = attend(
        ((1, 4), (1, 5), (1, 6), (3, 7), (3, 8)),
        (
            ((k1, None), (v31, None)),
            ((k1, None), (v13, None)),
            both(edge),
            ((k3, None), (v31, None)),
            ((k3, None), (edge, 1)),
        ),
        state,
        True,
    )
    returned = swap(sent, 1)
    self_out = jnp.where(
        core == 0,
        jnp.concatenate([kept, returned], axis=1),
        jnp.concatenate([returned, kept], axis=1),
    )
    return self_out, cross_out


def solution(mesh):
    rows = P(("ctx", "nbr"), "mp")
    pool = P(("ctx", "nbr"), None, "mp")
    return jax.shard_map(
        shards,
        mesh=mesh,
        in_specs=(rows, rows, rows, rows, pool, pool, P(), P()),
        out_specs=(rows, rows),
        check_vma=False,
    )
```

```python
import functools
import jax
import jax.numpy as jnp
from jax import lax
from jax.experimental import pallas as pl
from jax.experimental.pallas import tpu as pltpu
from jax.sharding import PartitionSpec as P

HD = 128
STRETCH = 64
LOG2E = 1.4426950408889634
EXP_SCALE = LOG2E * HD**-0.5
HIDDEN = -1e30
FLOOR = -1e29
ALL = ("ctx", "nbr")
RUN = 8
SMALL = pl.CostEstimate(flops=1, bytes_accessed=1, transcendentals=0)
LARGE = pl.CostEstimate(flops=10**11, bytes_accessed=10**8, transcendentals=0)


def place(d):
    return d // 4 % RUN, d // 2 % 2


def shift(value, by, to=lambda low, high: True):
    count = lax.axis_size(ALL)
    pairs = [(d, (d + by) % count) for d in range(count)]
    return lax.ppermute(value, ALL, [(a, b) for a, b in pairs if to(*place(b))])


def swap(value, bit):
    count = lax.axis_size(ALL)
    return lax.ppermute(value, ALL, [(d, d ^ bit) for d in range(count)])


def around(value, by):
    count = lax.axis_size(ALL)

    def target(d):
        low, high = place(d)
        z = (high * RUN + low + by) % (2 * RUN)
        return d + (z % RUN - low) * 4 + (z // RUN - high) * 2

    return lax.ppermute(value, ALL, [(d, target(d)) for d in range(count)])


def held_back(value, after):
    hbm = pl.BlockSpec(memory_space=pl.ANY)
    return pl.pallas_call(
        lambda *refs: None,
        in_specs=[hbm] * (1 + len(after)),
        out_specs=hbm,
        out_shape=jax.ShapeDtypeStruct(value.shape, value.dtype),
        input_output_aliases={0: 0},
        cost_estimate=SMALL,
    )(value, *after)


def self_kernel(blocks, first, last, skip, meta, *refs):
    refs = list(refs)
    q_ref = refs.pop(0)
    start_ref = refs.pop(0)
    pairs = [refs.pop(0) for _ in blocks]
    if not first:
        acc_in, top_in, total_in = refs.pop(0), refs.pop(0), refs.pop(0)
    refs = refs[skip:]
    if last:
        kept_ref, sent_ref = refs.pop(0), refs.pop(0)
    acc, top, total = refs
    rows = q_ref.shape[0]
    half = rows // 2
    if first:
        acc[...] = jnp.zeros_like(acc)
        top[...] = jnp.full_like(top, FLOOR)
        total[...] = jnp.zeros_like(total)
    else:
        acc[...] = acc_in[...]
        top[...] = top_in[...]
        total[...] = total_in[...]
    for bi, (back, flag) in enumerate(blocks):
        away = back * rows
        chip_first = jnp.minimum(meta[0], meta[1])
        seen = (chip_first - away + rows - 1 >= meta[2]) & (chip_first >= away)
        if flag:
            seen &= meta[2 + flag] > 0
        for qi in range(2):

            @pl.when(seen)
            def _(qi=qi, bi=bi, away=away):
                mine = pl.ds(qi * half, half)
                scores = lax.dot_general(
                    q_ref[mine, :],
                    pairs[bi][0],
                    (((1,), (1,)), ((), ())),
                    preferred_element_type=jnp.float32,
                )
                spot = lax.broadcasted_iota(jnp.int32, (half, half), 1)
                k_pos = jnp.concatenate([spot + meta[0], spot + meta[1]], axis=1) - away
                q_pos = meta[qi] + lax.broadcasted_iota(jnp.int32, (half, rows), 0)
                begin = jnp.concatenate([start_ref[mine, :]] * (rows // HD), axis=1)
                scores = jnp.where((k_pos <= q_pos) & (k_pos >= begin), scores, HIDDEN)
                old = top[0, mine, :]
                new = jnp.maximum(old, jnp.max(scores, axis=1, keepdims=True))
                wide = jnp.concatenate([new] * (rows // HD), axis=1)
                weights = jnp.exp2((scores - wide) * EXP_SCALE)
                factor = jnp.exp2((old - new) * EXP_SCALE)
                top[0, mine, :] = new
                total[0, mine, :] = total[0, mine, :] * factor + jnp.sum(
                    weights, axis=1, keepdims=True
                )
                acc[mine, :] = acc[mine, :] * factor + jnp.dot(
                    weights.astype(jnp.bfloat16), pairs[bi][1], preferred_element_type=jnp.float32
                )

    if last:
        out = (acc[...] / total[0]).astype(kept_ref.dtype)
        kept_ref[...] = out[:half]
        sent_ref[...] = out[half:]


def self_part(meta, queries, starts, blocks, pairs, state, last, after, cost):
    rows, width = queries.shape
    heads = width // HD
    column = pl.BlockSpec((rows, HD), lambda h: (0, h))
    pair = pl.BlockSpec((2, rows, HD), lambda h: (0, 0, h))
    stat = pl.BlockSpec((1, rows, HD), lambda h: (h, 0, 0))
    first = state is None
    in_specs = [
        pl.BlockSpec(memory_space=pltpu.SMEM),
        column,
        pl.BlockSpec((rows, HD), lambda h: (0, 0)),
    ] + [pair] * len(blocks)
    args = [meta, queries, starts, *pairs]
    if not first:
        in_specs += [column, stat, stat]
        args += list(state)
    in_specs += [pl.BlockSpec(memory_space=pl.ANY)] * len(after)
    args += list(after)
    if last:
        out_shape = (jax.ShapeDtypeStruct((rows // 2, width), jnp.bfloat16),) * 2
        out_specs = (pl.BlockSpec((rows // 2, HD), lambda h: (0, h)),) * 2
        scratch = [
            pltpu.VMEM((rows, HD), jnp.float32),
            pltpu.VMEM((1, rows, HD), jnp.float32),
            pltpu.VMEM((1, rows, HD), jnp.float32),
        ]
    else:
        out_shape = (
            jax.ShapeDtypeStruct((rows, width), jnp.float32),
            jax.ShapeDtypeStruct((heads, rows, HD), jnp.float32),
            jax.ShapeDtypeStruct((heads, rows, HD), jnp.float32),
        )
        out_specs = (column, stat, stat)
        scratch = []
    return pl.pallas_call(
        functools.partial(self_kernel, tuple(blocks), first, last, len(after)),
        grid=(heads,),
        in_specs=in_specs,
        out_specs=out_specs,
        out_shape=out_shape,
        scratch_shapes=scratch,
        compiler_params=pltpu.CompilerParams(vmem_limit_bytes=32 * 1024 * 1024),
        cost_estimate=cost,
    )(*args)


def cross_kernel(per, travels, meta, q_ref, k_here, v_here, side, *refs):
    if travels:
        o_ref, column = refs[-2:]
    else:
        o_ref, stat_ref, column = refs[-3:]
    k_side, v_side = side.at[0], side.at[1]
    length = k_here.shape[1]
    rows, width = q_ref.shape
    heads = width // HD
    requests = 2 * per

    def pick(here, side, r, cols):
        slot, beside = meta[r], meta[requests + r]
        return jnp.where(beside > 0, side[slot, :, cols], here[slot, :, cols])

    shape = (STRETCH, 2 * length)
    first = lax.broadcasted_iota(jnp.int32, shape, 1) < length
    have = jnp.concatenate(
        [
            jnp.where(first, meta[2 * requests + 2 * t], meta[2 * requests + 2 * t + 1])
            for t in range(per)
        ],
        axis=0,
    )
    lane = lax.broadcasted_iota(jnp.int32, (rows, HD), 1)
    stats = jnp.zeros((rows, HD), jnp.float32)
    for h in range(heads):
        cols = slice(h * HD, (h + 1) * HD)
        scores = []
        for t in range(per):
            keys = jnp.concatenate([pick(k_here, k_side, 2 * t + j, cols) for j in range(2)], axis=0)
            scores.append(
                lax.dot_general(
                    q_ref[t * STRETCH : (t + 1) * STRETCH, cols],
                    keys,
                    (((1,), (1,)), ((), ())),
                    preferred_element_type=jnp.float32,
                )
            )
        scores = jnp.where(have > 0, jnp.concatenate(scores, axis=0), HIDDEN)
        top = jnp.maximum(jnp.max(scores, axis=1, keepdims=True), FLOOR)
        weights = jnp.exp2((scores - top) * EXP_SCALE)
        total = jnp.sum(weights, axis=1, keepdims=True)
        weights = weights.astype(jnp.bfloat16)
        stats = jnp.where(lane == h, top, jnp.where(lane == heads + h, total, stats))
        for t in range(per):
            values = jnp.concatenate([pick(v_here, v_side, 2 * t + j, cols) for j in range(2)], axis=0)
            o_ref[t * STRETCH : (t + 1) * STRETCH, cols] = jnp.dot(
                weights[t * STRETCH : (t + 1) * STRETCH],
                values,
                preferred_element_type=jnp.float32,
            ).astype(o_ref.dtype)
    column[...] = stats
    stats = jnp.transpose(column[...])[: 2 * heads, :]
    if travels:
        for i in range(3):
            piece = stats.astype(jnp.bfloat16)
            o_ref[rows : rows + 2 * heads, i * rows : (i + 1) * rows] = piece
            stats = stats - piece.astype(jnp.float32)
        o_ref[rows : rows + 2 * heads, 3 * rows :] = jnp.zeros(
            (2 * heads, width - 3 * rows), jnp.bfloat16
        )
    else:
        stat_ref[...] = stats


def cross_part(meta, queries, pool, travels, after, cost):
    rows, width = queries.shape
    heads = width // HD
    vmem = pl.BlockSpec(memory_space=pltpu.VMEM)
    if travels:
        out_specs = vmem
        out_shape = jax.ShapeDtypeStruct((rows + 2 * heads, width), jnp.bfloat16)
    else:
        out_specs = (vmem, vmem)
        out_shape = (
            jax.ShapeDtypeStruct((rows, width), jnp.float32),
            jax.ShapeDtypeStruct((2 * heads, rows), jnp.float32),
        )
    return pl.pallas_call(
        functools.partial(cross_kernel, rows // STRETCH, travels),
        in_specs=[pl.BlockSpec(memory_space=pltpu.SMEM)]
        + [vmem] * 4
        + [pl.BlockSpec(memory_space=pl.ANY)] * len(after),
        out_specs=out_specs,
        out_shape=out_shape,
        scratch_shapes=[pltpu.VMEM((rows, HD), jnp.float32)],
        compiler_params=pltpu.CompilerParams(vmem_limit_bytes=32 * 1024 * 1024),
        cost_estimate=cost,
    )(meta, queries, *pool, *after)


def merge_kernel(oa_ref, ob_ref, sa_ref, out_ref):
    rows, width = oa_ref.shape
    heads = width // HD
    pieces = ob_ref[rows : rows + 2 * heads, : 3 * rows].astype(jnp.float32)
    far = pieces[:, :rows] + pieces[:, rows : 2 * rows] + pieces[:, 2 * rows :]
    fill = jnp.zeros((HD - 4 * heads, rows), jnp.float32)
    stats = jnp.transpose(jnp.concatenate([sa_ref[...], far, fill], axis=0))
    for h in range(heads):
        cols = slice(h * HD, (h + 1) * HD)
        top_a, total_a, top_b, total_b = (
            stats[:, i * heads + h : i * heads + h + 1] for i in range(4)
        )
        top = jnp.maximum(top_a, top_b)
        part_a = jnp.exp2((top_a - top) * EXP_SCALE)
        part_b = jnp.exp2((top_b - top) * EXP_SCALE)
        share = 1.0 / (total_a * part_a + total_b * part_b)
        out_ref[:, cols] = (
            oa_ref[:, cols] * (part_a * share)
            + ob_ref[:rows, cols].astype(jnp.float32) * (part_b * share)
        ).astype(out_ref.dtype)


def merge(oa, ob, sa):
    rows, width = oa.shape
    vmem = pl.BlockSpec(memory_space=pltpu.VMEM)
    return pl.pallas_call(
        merge_kernel,
        in_specs=[vmem] * 3,
        out_specs=vmem,
        out_shape=jax.ShapeDtypeStruct((rows, width), jnp.bfloat16),
        compiler_params=pltpu.CompilerParams(vmem_limit_bytes=32 * 1024 * 1024),
        cost_estimate=SMALL,
    )(oa, ob, sa)


def shards(
    self_queries,
    self_keys,
    self_values,
    cross_queries,
    neighbour_keys,
    neighbour_values,
    neighbour_table,
    doc_lengths,
):
    tokens, width = self_queries.shape
    part = width // 2
    device = lax.axis_index(ALL)
    core = device % 2
    zhi = (device // 2) % 2
    chip = device // 2


    def mine(x):
        return lax.dynamic_slice_in_dim(x, core * part, part, 1)

    def other(x):
        return lax.dynamic_slice_in_dim(x, (1 - core) * part, part, 1)

    trio = (self_keys, self_values, self_queries)
    beside = swap(jnp.stack([other(x) for x in trio]), 1)
    kv0 = jnp.stack([jnp.concatenate([mine(x), beside[i]]) for i, x in enumerate(trio[:2])])
    q0 = jnp.concatenate([mine(self_queries), beside[2]])
    pool = held_back(jnp.stack([neighbour_keys, neighbour_values]), (kv0,))
    pool_beside = swap(pool, 1)

    base = jnp.stack([chip * 2 * tokens + core * tokens, chip * 2 * tokens + (1 - core) * tokens])
    positions = (base[:, None] + jnp.arange(tokens, dtype=jnp.int32)[None, :]).reshape(-1)
    ends = jnp.cumsum(doc_lengths)
    starts = jnp.sum(jnp.where(ends[None, :] <= positions[:, None], doc_lengths[None, :], 0), axis=1)
    low, high = place(device)
    first_a, first_b = (low == 0) & (high == 0), (low == 0) & (high == 1)
    flags = [low > 0, first_b, first_a, low < RUN - 1, low == RUN - 1]
    self_meta = jnp.stack(
        [base[0], base[1], jnp.minimum(starts[0], starts[tokens]), *flags], dtype=jnp.int32
    )
    starts_wide = jnp.broadcast_to(starts[:, None], (2 * tokens, HD)).astype(jnp.int32)

    def attend(blocks, pairs, state, last=False, after=(), cost=SMALL):
        return self_part(
            self_meta, q0, starts_wide, blocks, pairs, state, last, after, cost
        )

    far_queries = around(cross_queries, 1)

    kv3 = shift(kv0, 6)
    kv2 = shift(kv0, 4)
    kv4_far = shift(kv0, 8, lambda low, high: low == 0 and high == 1)

    state = attend(((0, 0),), (kv0,), None, cost=LARGE)
    far_queries = around(held_back(far_queries, state[:1]), 7)
    def pool_meta(owner):
        per = tokens // STRETCH
        ids = lax.dynamic_slice_in_dim(neighbour_table, owner * per, per, 0).reshape(-1)
        holder, slot = ids // neighbour_keys.shape[0], ids % neighbour_keys.shape[0]
        return jnp.concatenate([slot, holder % 2 != core, holder // 2 == zhi]).astype(jnp.int32)

    pool = (neighbour_keys, neighbour_values, pool_beside)
    near_sum, near_stat = cross_part(
        pool_meta(device), cross_queries, pool, False, state[:1], SMALL
    )
    far_sum = cross_part(
        pool_meta(device ^ 2), far_queries, pool, True, (near_stat,), SMALL
    )
    back_sum = swap(far_sum, 2)
    kv2 = held_back(kv2, (far_sum,))
    kv4 = shift(kv2, 4, lambda low, high: low > 0)
    kv1_edge = lax.ppermute(
        jnp.where(high == 0, kv2, kv4_far),
        ALL,
        [
            (d, (d - 2 - 4 * place(d)[1]) % lax.axis_size(ALL))
            for d in range(lax.axis_size(ALL))
            if place(d)[0] == 0
        ],
    )
    state = attend(
        ((2, 0), (4, 1), (4, 2)),
        (kv2, kv4, kv4_far),
        state,
        after=(far_sum,),
    )
    kv3 = held_back(kv3, (kv2,))
    kv1 = shift(kv3, -4, lambda low, high: low < RUN - 1)
    kv4_last = shift(kv3, 2, lambda low, high: low == 0 and high == 0)
    state = attend(((3, 0),), (kv3,), state)
    kept, sent = attend(((4, 3), (1, 4), (1, 5)), (kv4_last, kv1, kv1_edge), state, True)
    returned = swap(sent, 1)
    self_out = jnp.where(
        core == 0,
        jnp.concatenate([kept, returned], axis=1),
        jnp.concatenate([returned, kept], axis=1),
    )
    cross_out = merge(near_sum, back_sum, near_stat)
    return self_out, cross_out


def solution(mesh):
    rows = P(("ctx", "nbr"), "mp")
    pool = P(("ctx", "nbr"), None, "mp")
    return jax.shard_map(
        shards,
        mesh=mesh,
        in_specs=(rows, rows, rows, rows, pool, pool, P(), P()),
        out_specs=(rows, rows),
        check_vma=False,
    )
```

```python
import functools
import jax
import jax.numpy as jnp
from jax import lax
from jax.experimental import pallas as pl
from jax.experimental.pallas import tpu as pltpu
from jax.sharding import PartitionSpec as P

HD = 128
STRETCH = 64
LOG2E = 1.4426950408889634
EXP_SCALE = LOG2E * HD**-0.5
HIDDEN = -1e30
FLOOR = -1e29
ALL = ("ctx", "nbr")
RUN = 8
SMALL = pl.CostEstimate(flops=1, bytes_accessed=1, transcendentals=0)
LARGE = pl.CostEstimate(flops=10**11, bytes_accessed=10**8, transcendentals=0)


def place(d):
    return d // 4 % RUN, d // 2 % 2


def shift(value, by, to=lambda low, high: True):
    count = lax.axis_size(ALL)
    pairs = [(d, (d + by) % count) for d in range(count)]
    return lax.ppermute(value, ALL, [(a, b) for a, b in pairs if to(*place(b))])


def swap(value, bit):
    count = lax.axis_size(ALL)
    return lax.ppermute(value, ALL, [(d, d ^ bit) for d in range(count)])


def around(value, by):
    count = lax.axis_size(ALL)

    def target(d):
        low, high = place(d)
        z = (high * RUN + low + by) % (2 * RUN)
        return d + (z % RUN - low) * 4 + (z // RUN - high) * 2

    return lax.ppermute(value, ALL, [(d, target(d)) for d in range(count)])


def held_back(value, after):
    hbm = pl.BlockSpec(memory_space=pl.ANY)
    return pl.pallas_call(
        lambda *refs: None,
        in_specs=[hbm] * (1 + len(after)),
        out_specs=hbm,
        out_shape=jax.ShapeDtypeStruct(value.shape, value.dtype),
        input_output_aliases={0: 0},
        cost_estimate=SMALL,
    )(value, *after)


def cut_kernel(core, a_ref, b_ref, c_ref, out_ref):
    out_ref[0] = a_ref[...]
    out_ref[1] = b_ref[...]
    out_ref[2] = c_ref[...]


def cut(core, arrays):
    rows, width = arrays[0].shape
    part = width // 2
    return pl.pallas_call(
        cut_kernel,
        grid_spec=pltpu.PrefetchScalarGridSpec(
            num_scalar_prefetch=1,
            grid=(1,),
            in_specs=[pl.BlockSpec((rows, part), lambda i, c: (0, 1 - c[0]))] * 3,
            out_specs=pl.BlockSpec((3, rows, part), lambda i, c: (0, 0, 0)),
        ),
        out_shape=jax.ShapeDtypeStruct((3, rows, part), arrays[0].dtype),
        cost_estimate=SMALL,
    )(core, *arrays)


def join_kernel(core, a_ref, b_ref, c_ref, beside_ref, pair_ref, single_ref):
    rows = a_ref.shape[0]
    for i, ref in enumerate((a_ref, b_ref)):
        pair_ref[i, :rows] = ref[...]
        pair_ref[i, rows:] = beside_ref[i]
    single_ref[:rows] = c_ref[...]
    single_ref[rows:] = beside_ref[2]


def join(core, arrays, beside):
    rows, width = arrays[0].shape
    part = width // 2
    dtype = arrays[0].dtype
    return pl.pallas_call(
        join_kernel,
        grid_spec=pltpu.PrefetchScalarGridSpec(
            num_scalar_prefetch=1,
            grid=(1,),
            in_specs=[pl.BlockSpec((rows, part), lambda i, c: (0, c[0]))] * 3
            + [pl.BlockSpec((3, rows, part), lambda i, c: (0, 0, 0))],
            out_specs=(
                pl.BlockSpec((2, 2 * rows, part), lambda i, c: (0, 0, 0)),
                pl.BlockSpec((2 * rows, part), lambda i, c: (0, 0)),
            ),
        ),
        out_shape=(
            jax.ShapeDtypeStruct((2, 2 * rows, part), dtype),
            jax.ShapeDtypeStruct((2 * rows, part), dtype),
        ),
        compiler_params=pltpu.CompilerParams(vmem_limit_bytes=32 * 1024 * 1024),
        cost_estimate=SMALL,
    )(core, *arrays, beside)


def self_kernel(blocks, first, last, skip, meta, *refs):
    refs = list(refs)
    q_ref = refs.pop(0)
    start_ref = refs.pop(0)
    pairs = [refs.pop(0) for _ in blocks]
    if not first:
        acc_in, top_in, total_in = refs.pop(0), refs.pop(0), refs.pop(0)
    refs = refs[skip:]
    if last:
        kept_ref, sent_ref = refs.pop(0), refs.pop(0)
    acc, top, total = refs
    rows = q_ref.shape[0]
    half = rows // 2
    if first:
        acc[...] = jnp.zeros_like(acc)
        top[...] = jnp.full_like(top, FLOOR)
        total[...] = jnp.zeros_like(total)
    else:
        acc[...] = acc_in[...]
        top[...] = top_in[...]
        total[...] = total_in[...]
    for bi, (back, flag) in enumerate(blocks):
        away = back * rows
        chip_first = jnp.minimum(meta[0], meta[1])
        seen = (chip_first - away + rows - 1 >= meta[2]) & (chip_first >= away)
        if flag:
            seen &= meta[2 + flag] > 0
        for qi in range(2):

            @pl.when(seen)
            def _(qi=qi, bi=bi, away=away):
                mine = pl.ds(qi * half, half)
                scores = lax.dot_general(
                    q_ref[mine, :],
                    pairs[bi][0],
                    (((1,), (1,)), ((), ())),
                    preferred_element_type=jnp.float32,
                )
                spot = lax.broadcasted_iota(jnp.int32, (half, half), 1)
                k_pos = jnp.concatenate([spot + meta[0], spot + meta[1]], axis=1) - away
                q_pos = meta[qi] + lax.broadcasted_iota(jnp.int32, (half, rows), 0)
                begin = jnp.concatenate([start_ref[mine, :]] * (rows // HD), axis=1)
                scores = jnp.where((k_pos <= q_pos) & (k_pos >= begin), scores, HIDDEN)
                old = top[0, mine, :]
                new = jnp.maximum(old, jnp.max(scores, axis=1, keepdims=True))
                wide = jnp.concatenate([new] * (rows // HD), axis=1)
                weights = jnp.exp2((scores - wide) * EXP_SCALE)
                factor = jnp.exp2((old - new) * EXP_SCALE)
                top[0, mine, :] = new
                total[0, mine, :] = total[0, mine, :] * factor + jnp.sum(
                    weights, axis=1, keepdims=True
                )
                acc[mine, :] = acc[mine, :] * factor + jnp.dot(
                    weights.astype(jnp.bfloat16), pairs[bi][1], preferred_element_type=jnp.float32
                )

    if last:
        out = (acc[...] / total[0]).astype(kept_ref.dtype)
        kept_ref[...] = out[:half]
        sent_ref[...] = out[half:]


def self_part(meta, queries, starts, blocks, pairs, state, last, after, cost):
    rows, width = queries.shape
    heads = width // HD
    column = pl.BlockSpec((rows, HD), lambda h: (0, h))
    pair = pl.BlockSpec((2, rows, HD), lambda h: (0, 0, h))
    stat = pl.BlockSpec((1, rows, HD), lambda h: (h, 0, 0))
    first = state is None
    in_specs = [
        pl.BlockSpec(memory_space=pltpu.SMEM),
        column,
        pl.BlockSpec((rows, HD), lambda h: (0, 0)),
    ] + [pair] * len(blocks)
    args = [meta, queries, starts, *pairs]
    if not first:
        in_specs += [column, stat, stat]
        args += list(state)
    in_specs += [pl.BlockSpec(memory_space=pl.ANY)] * len(after)
    args += list(after)
    if last:
        out_shape = (jax.ShapeDtypeStruct((rows // 2, width), jnp.bfloat16),) * 2
        out_specs = (pl.BlockSpec((rows // 2, HD), lambda h: (0, h)),) * 2
        scratch = [
            pltpu.VMEM((rows, HD), jnp.float32),
            pltpu.VMEM((1, rows, HD), jnp.float32),
            pltpu.VMEM((1, rows, HD), jnp.float32),
        ]
    else:
        out_shape = (
            jax.ShapeDtypeStruct((rows, width), jnp.float32),
            jax.ShapeDtypeStruct((heads, rows, HD), jnp.float32),
            jax.ShapeDtypeStruct((heads, rows, HD), jnp.float32),
        )
        out_specs = (column, stat, stat)
        scratch = []
    return pl.pallas_call(
        functools.partial(self_kernel, tuple(blocks), first, last, len(after)),
        grid=(heads,),
        in_specs=in_specs,
        out_specs=out_specs,
        out_shape=out_shape,
        scratch_shapes=scratch,
        compiler_params=pltpu.CompilerParams(vmem_limit_bytes=32 * 1024 * 1024),
        cost_estimate=cost,
    )(*args)


def cross_kernel(per, travels, meta, q_ref, k_here, v_here, side, *refs):
    if travels:
        o_ref, column = refs[-2:]
    else:
        o_ref, stat_ref, column = refs[-3:]
    k_side, v_side = side.at[0], side.at[1]
    length = k_here.shape[1]
    rows, width = q_ref.shape
    heads = width // HD
    requests = 2 * per

    def pick(here, side, r, cols):
        slot, beside = meta[r], meta[requests + r]
        return jnp.where(beside > 0, side[slot, :, cols], here[slot, :, cols])

    shape = (STRETCH, 2 * length)
    first = lax.broadcasted_iota(jnp.int32, shape, 1) < length
    have = jnp.concatenate(
        [
            jnp.where(first, meta[2 * requests + 2 * t], meta[2 * requests + 2 * t + 1])
            for t in range(per)
        ],
        axis=0,
    )
    lane = lax.broadcasted_iota(jnp.int32, (rows, HD), 1)
    stats = jnp.zeros((rows, HD), jnp.float32)
    for h in range(heads):
        cols = slice(h * HD, (h + 1) * HD)
        scores = []
        for t in range(per):
            keys = jnp.concatenate([pick(k_here, k_side, 2 * t + j, cols) for j in range(2)], axis=0)
            scores.append(
                lax.dot_general(
                    q_ref[t * STRETCH : (t + 1) * STRETCH, cols],
                    keys,
                    (((1,), (1,)), ((), ())),
                    preferred_element_type=jnp.float32,
                )
            )
        scores = jnp.where(have > 0, jnp.concatenate(scores, axis=0), HIDDEN)
        top = jnp.maximum(jnp.max(scores, axis=1, keepdims=True), FLOOR)
        weights = jnp.exp2((scores - top) * EXP_SCALE)
        total = jnp.sum(weights, axis=1, keepdims=True)
        weights = weights.astype(jnp.bfloat16)
        stats = jnp.where(lane == h, top, jnp.where(lane == heads + h, total, stats))
        for t in range(per):
            values = jnp.concatenate([pick(v_here, v_side, 2 * t + j, cols) for j in range(2)], axis=0)
            o_ref[t * STRETCH : (t + 1) * STRETCH, cols] = jnp.dot(
                weights[t * STRETCH : (t + 1) * STRETCH],
                values,
                preferred_element_type=jnp.float32,
            ).astype(o_ref.dtype)
    column[...] = stats
    stats = jnp.transpose(column[...])[: 2 * heads, :]
    if travels:
        for i in range(3):
            piece = stats.astype(jnp.bfloat16)
            o_ref[rows : rows + 2 * heads, i * rows : (i + 1) * rows] = piece
            stats = stats - piece.astype(jnp.float32)
        o_ref[rows : rows + 2 * heads, 3 * rows :] = jnp.zeros(
            (2 * heads, width - 3 * rows), jnp.bfloat16
        )
    else:
        stat_ref[...] = stats


def cross_part(meta, queries, pool, travels, after, cost):
    rows, width = queries.shape
    heads = width // HD
    vmem = pl.BlockSpec(memory_space=pltpu.VMEM)
    if travels:
        out_specs = vmem
        out_shape = jax.ShapeDtypeStruct((rows + 2 * heads, width), jnp.bfloat16)
    else:
        out_specs = (vmem, vmem)
        out_shape = (
            jax.ShapeDtypeStruct((rows, width), jnp.float32),
            jax.ShapeDtypeStruct((2 * heads, rows), jnp.float32),
        )
    return pl.pallas_call(
        functools.partial(cross_kernel, rows // STRETCH, travels),
        in_specs=[pl.BlockSpec(memory_space=pltpu.SMEM)]
        + [vmem] * 4
        + [pl.BlockSpec(memory_space=pl.ANY)] * len(after),
        out_specs=out_specs,
        out_shape=out_shape,
        scratch_shapes=[pltpu.VMEM((rows, HD), jnp.float32)],
        compiler_params=pltpu.CompilerParams(vmem_limit_bytes=32 * 1024 * 1024),
        cost_estimate=cost,
    )(meta, queries, *pool, *after)


def merge_kernel(oa_ref, ob_ref, sa_ref, out_ref):
    rows, width = oa_ref.shape
    heads = width // HD
    pieces = ob_ref[rows : rows + 2 * heads, : 3 * rows].astype(jnp.float32)
    far = pieces[:, :rows] + pieces[:, rows : 2 * rows] + pieces[:, 2 * rows :]
    fill = jnp.zeros((HD - 4 * heads, rows), jnp.float32)
    stats = jnp.transpose(jnp.concatenate([sa_ref[...], far, fill], axis=0))
    for h in range(heads):
        cols = slice(h * HD, (h + 1) * HD)
        top_a, total_a, top_b, total_b = (
            stats[:, i * heads + h : i * heads + h + 1] for i in range(4)
        )
        top = jnp.maximum(top_a, top_b)
        part_a = jnp.exp2((top_a - top) * EXP_SCALE)
        part_b = jnp.exp2((top_b - top) * EXP_SCALE)
        share = 1.0 / (total_a * part_a + total_b * part_b)
        out_ref[:, cols] = (
            oa_ref[:, cols] * (part_a * share)
            + ob_ref[:rows, cols].astype(jnp.float32) * (part_b * share)
        ).astype(out_ref.dtype)


def merge(oa, ob, sa):
    rows, width = oa.shape
    vmem = pl.BlockSpec(memory_space=pltpu.VMEM)
    return pl.pallas_call(
        merge_kernel,
        in_specs=[vmem] * 3,
        out_specs=vmem,
        out_shape=jax.ShapeDtypeStruct((rows, width), jnp.bfloat16),
        compiler_params=pltpu.CompilerParams(vmem_limit_bytes=32 * 1024 * 1024),
        cost_estimate=SMALL,
    )(oa, ob, sa)


def shards(
    self_queries,
    self_keys,
    self_values,
    cross_queries,
    neighbour_keys,
    neighbour_values,
    neighbour_table,
    doc_lengths,
):
    tokens, width = self_queries.shape
    part = width // 2
    device = lax.axis_index(ALL)
    core = device % 2
    zhi = (device // 2) % 2
    chip = device // 2

    far_queries = swap(cross_queries, 2)

    which = core.astype(jnp.int32).reshape(1)
    trio = (self_keys, self_values, self_queries)
    beside = swap(cut(which, trio), 1)
    kv0, q0 = join(which, trio, beside)
    pool = held_back(jnp.stack([neighbour_keys, neighbour_values]), (kv0,))
    pool_beside = swap(pool, 1)

    base = jnp.stack([chip * 2 * tokens + core * tokens, chip * 2 * tokens + (1 - core) * tokens])
    positions = (base[:, None] + jnp.arange(tokens, dtype=jnp.int32)[None, :]).reshape(-1)
    ends = jnp.cumsum(doc_lengths)
    starts = jnp.sum(jnp.where(ends[None, :] <= positions[:, None], doc_lengths[None, :], 0), axis=1)
    low, high = place(device)
    flags = [
        low > 0,
        (low == 0) & (high == 1),
        (low == 0) & (high == 0),
        low < RUN - 1,
        low == RUN - 1,
    ]
    self_meta = jnp.stack(
        [base[0], base[1], jnp.minimum(starts[0], starts[tokens]), *flags], dtype=jnp.int32
    )
    starts_wide = jnp.broadcast_to(starts[:, None], (2 * tokens, HD)).astype(jnp.int32)

    def attend(blocks, pairs, state, last=False, after=(), cost=SMALL):
        return self_part(
            self_meta, q0, starts_wide, blocks, pairs, state, last, after, cost
        )

    kv3 = shift(kv0, 6)
    kv2 = shift(kv0, 4)
    kv4_far = shift(kv0, 8, lambda low, high: low == 0 and high == 1)

    state = attend(((0, 0),), (kv0,), None, cost=LARGE)
    def pool_meta(owner):
        per = tokens // STRETCH
        ids = lax.dynamic_slice_in_dim(neighbour_table, owner * per, per, 0).reshape(-1)
        holder, slot = ids // neighbour_keys.shape[0], ids % neighbour_keys.shape[0]
        return jnp.concatenate([slot, holder % 2 != core, holder // 2 == zhi]).astype(jnp.int32)

    pool = (neighbour_keys, neighbour_values, pool_beside)
    near_sum, near_stat = cross_part(
        pool_meta(device), cross_queries, pool, False, state[:1], SMALL
    )
    far_sum = cross_part(
        pool_meta(device ^ 2), far_queries, pool, True, (near_stat,), SMALL
    )
    nearly = around(far_sum, 7)
    kv2 = held_back(kv2, (nearly,))
    kv4 = shift(kv2, 4, lambda low, high: low > 0)
    kv1_edge = lax.ppermute(
        jnp.where(high == 0, kv2, kv4_far),
        ALL,
        [
            (d, (d - 2 - 4 * place(d)[1]) % lax.axis_size(ALL))
            for d in range(lax.axis_size(ALL))
            if place(d)[0] == 0
        ],
    )
    state = attend(((2, 0),), (kv2,), state)
    kv3 = held_back(kv3, (kv2, state[0]))
    kv1 = shift(kv3, -4, lambda low, high: low < RUN - 1)
    kv4_last = shift(kv3, 2, lambda low, high: low == 0 and high == 0)
    back_sum = around(nearly, 1)
    state = attend(((4, 1), (4, 2), (3, 0)), (kv4, kv4_far, kv3), state)
    kept, sent = attend(((4, 3), (1, 4), (1, 5)), (kv4_last, kv1, kv1_edge), state, True)
    returned = swap(sent, 1)
    self_out = jnp.where(
        core == 0,
        jnp.concatenate([kept, returned], axis=1),
        jnp.concatenate([returned, kept], axis=1),
    )
    cross_out = merge(near_sum, back_sum, near_stat)
    return self_out, cross_out


def solution(mesh):
    rows = P(("ctx", "nbr"), "mp")
    pool = P(("ctx", "nbr"), None, "mp")
    return jax.shard_map(
        shards,
        mesh=mesh,
        in_specs=(rows, rows, rows, rows, pool, pool, P(), P()),
        out_specs=(rows, rows),
        check_vma=False,
    )
```

```python
import functools
import jax
import jax.numpy as jnp
from jax import lax
from jax.experimental import pallas as pl
from jax.experimental.pallas import tpu as pltpu
from jax.sharding import PartitionSpec as P

HD = 128
STRETCH = 64
LOG2E = 1.4426950408889634
EXP_SCALE = LOG2E * HD**-0.5
HIDDEN = -1e30
FLOOR = -1e29
ALL = ("ctx", "nbr")
RUN = 8
SMALL = pl.CostEstimate(flops=1, bytes_accessed=1, transcendentals=0)
LARGE = pl.CostEstimate(flops=10**11, bytes_accessed=10**8, transcendentals=0)


def place(d):
    return d // 4 % RUN, d // 2 % 2


def shift(value, by, to=lambda low, high: True):
    count = lax.axis_size(ALL)
    pairs = [(d, (d + by) % count) for d in range(count)]
    return lax.ppermute(value, ALL, [(a, b) for a, b in pairs if to(*place(b))])


def swap(value, bit):
    count = lax.axis_size(ALL)
    return lax.ppermute(value, ALL, [(d, d ^ bit) for d in range(count)])


def around(value, by):
    count = lax.axis_size(ALL)

    def target(d):
        low, high = place(d)
        z = (high * RUN + low + by) % (2 * RUN)
        return d + (z % RUN - low) * 4 + (z // RUN - high) * 2

    return lax.ppermute(value, ALL, [(d, target(d)) for d in range(count)])


def held_back(value, after):
    hbm = pl.BlockSpec(memory_space=pl.ANY)
    return pl.pallas_call(
        lambda *refs: None,
        in_specs=[hbm] * (1 + len(after)),
        out_specs=hbm,
        out_shape=jax.ShapeDtypeStruct(value.shape, value.dtype),
        input_output_aliases={0: 0},
        cost_estimate=SMALL,
    )(value, *after)


def cut_kernel(core, a_ref, b_ref, c_ref, out_ref):
    out_ref[0] = a_ref[...]
    out_ref[1] = b_ref[...]
    out_ref[2] = c_ref[...]


def cut(core, arrays):
    rows, width = arrays[0].shape
    part = width // 2
    return pl.pallas_call(
        cut_kernel,
        grid_spec=pltpu.PrefetchScalarGridSpec(
            num_scalar_prefetch=1,
            grid=(1,),
            in_specs=[pl.BlockSpec((rows, part), lambda i, c: (0, 1 - c[0]))] * 3,
            out_specs=pl.BlockSpec((3, rows, part), lambda i, c: (0, 0, 0)),
        ),
        out_shape=jax.ShapeDtypeStruct((3, rows, part), arrays[0].dtype),
        cost_estimate=SMALL,
    )(core, *arrays)


def join_kernel(core, a_ref, b_ref, c_ref, beside_ref, pair_ref, single_ref):
    rows = a_ref.shape[0]
    for i, ref in enumerate((a_ref, b_ref)):
        pair_ref[i, :rows] = ref[...]
        pair_ref[i, rows:] = beside_ref[i]
    single_ref[:rows] = c_ref[...]
    single_ref[rows:] = beside_ref[2]


def join(core, arrays, beside):
    rows, width = arrays[0].shape
    part = width // 2
    dtype = arrays[0].dtype
    return pl.pallas_call(
        join_kernel,
        grid_spec=pltpu.PrefetchScalarGridSpec(
            num_scalar_prefetch=1,
            grid=(1,),
            in_specs=[pl.BlockSpec((rows, part), lambda i, c: (0, c[0]))] * 3
            + [pl.BlockSpec((3, rows, part), lambda i, c: (0, 0, 0))],
            out_specs=(
                pl.BlockSpec((2, 2 * rows, part), lambda i, c: (0, 0, 0)),
                pl.BlockSpec((2 * rows, part), lambda i, c: (0, 0)),
            ),
        ),
        out_shape=(
            jax.ShapeDtypeStruct((2, 2 * rows, part), dtype),
            jax.ShapeDtypeStruct((2 * rows, part), dtype),
        ),
        compiler_params=pltpu.CompilerParams(vmem_limit_bytes=32 * 1024 * 1024),
        cost_estimate=SMALL,
    )(core, *arrays, beside)


def self_kernel(blocks, first, last, skip, meta, *refs):
    refs = list(refs)
    q_ref = refs.pop(0)
    start_ref = refs.pop(0)
    pairs = [refs.pop(0) for _ in blocks]
    if not first:
        acc_in, top_in, total_in = refs.pop(0), refs.pop(0), refs.pop(0)
    refs = refs[skip:]
    if last:
        kept_ref, sent_ref = refs.pop(0), refs.pop(0)
    acc, top, total = refs
    rows = q_ref.shape[0]
    half = rows // 2
    if first:
        acc[...] = jnp.zeros_like(acc)
        top[...] = jnp.full_like(top, FLOOR)
        total[...] = jnp.zeros_like(total)
    else:
        acc[...] = acc_in[...]
        top[...] = top_in[...]
        total[...] = total_in[...]
    for bi, (back, flag) in enumerate(blocks):
        away = back * rows
        chip_first = jnp.minimum(meta[0], meta[1])
        seen = (chip_first - away + rows - 1 >= meta[2]) & (chip_first >= away)
        if flag:
            seen &= meta[2 + flag] > 0
        for qi in range(2):

            @pl.when(seen)
            def _(qi=qi, bi=bi, away=away):
                mine = pl.ds(qi * half, half)
                scores = lax.dot_general(
                    q_ref[mine, :],
                    pairs[bi][0],
                    (((1,), (1,)), ((), ())),
                    preferred_element_type=jnp.float32,
                )
                spot = lax.broadcasted_iota(jnp.int32, (half, half), 1)
                k_pos = jnp.concatenate([spot + meta[0], spot + meta[1]], axis=1) - away
                q_pos = meta[qi] + lax.broadcasted_iota(jnp.int32, (half, rows), 0)
                begin = jnp.concatenate([start_ref[mine, :]] * (rows // HD), axis=1)
                scores = jnp.where((k_pos <= q_pos) & (k_pos >= begin), scores, HIDDEN)
                old = top[0, mine, :]
                new = jnp.maximum(old, jnp.max(scores, axis=1, keepdims=True))
                wide = jnp.concatenate([new] * (rows // HD), axis=1)
                weights = jnp.exp2((scores - wide) * EXP_SCALE)
                factor = jnp.exp2((old - new) * EXP_SCALE)
                top[0, mine, :] = new
                total[0, mine, :] = total[0, mine, :] * factor + jnp.sum(
                    weights, axis=1, keepdims=True
                )
                acc[mine, :] = acc[mine, :] * factor + jnp.dot(
                    weights.astype(jnp.bfloat16), pairs[bi][1], preferred_element_type=jnp.float32
                )

    if last:
        out = (acc[...] / total[0]).astype(kept_ref.dtype)
        kept_ref[...] = out[:half]
        sent_ref[...] = out[half:]


def self_part(meta, queries, starts, blocks, pairs, state, last, after, cost):
    rows, width = queries.shape
    heads = width // HD
    column = pl.BlockSpec((rows, HD), lambda h: (0, h))
    pair = pl.BlockSpec((2, rows, HD), lambda h: (0, 0, h))
    stat = pl.BlockSpec((1, rows, HD), lambda h: (h, 0, 0))
    first = state is None
    in_specs = [
        pl.BlockSpec(memory_space=pltpu.SMEM),
        column,
        pl.BlockSpec((rows, HD), lambda h: (0, 0)),
    ] + [pair] * len(blocks)
    args = [meta, queries, starts, *pairs]
    if not first:
        in_specs += [column, stat, stat]
        args += list(state)
    in_specs += [pl.BlockSpec(memory_space=pl.ANY)] * len(after)
    args += list(after)
    if last:
        out_shape = (jax.ShapeDtypeStruct((rows // 2, width), jnp.bfloat16),) * 2
        out_specs = (pl.BlockSpec((rows // 2, HD), lambda h: (0, h)),) * 2
        scratch = [
            pltpu.VMEM((rows, HD), jnp.float32),
            pltpu.VMEM((1, rows, HD), jnp.float32),
            pltpu.VMEM((1, rows, HD), jnp.float32),
        ]
    else:
        out_shape = (
            jax.ShapeDtypeStruct((rows, width), jnp.float32),
            jax.ShapeDtypeStruct((heads, rows, HD), jnp.float32),
            jax.ShapeDtypeStruct((heads, rows, HD), jnp.float32),
        )
        out_specs = (column, stat, stat)
        scratch = []
    return pl.pallas_call(
        functools.partial(self_kernel, tuple(blocks), first, last, len(after)),
        grid=(heads,),
        in_specs=in_specs,
        out_specs=out_specs,
        out_shape=out_shape,
        scratch_shapes=scratch,
        compiler_params=pltpu.CompilerParams(vmem_limit_bytes=32 * 1024 * 1024),
        cost_estimate=cost,
    )(*args)


def cross_kernel(per, travels, meta, q_ref, k_here, v_here, side, *refs):
    if travels:
        o_ref, column = refs[-2:]
    else:
        o_ref, stat_ref, column = refs[-3:]
    k_side, v_side = side.at[0], side.at[1]
    length = k_here.shape[1]
    rows, width = q_ref.shape
    heads = width // HD
    requests = 2 * per

    def pick(here, side, r, cols):
        slot, beside = meta[r], meta[requests + r]
        return jnp.where(beside > 0, side[slot, :, cols], here[slot, :, cols])

    shape = (STRETCH, 2 * length)
    first = lax.broadcasted_iota(jnp.int32, shape, 1) < length
    have = jnp.concatenate(
        [
            jnp.where(first, meta[2 * requests + 2 * t], meta[2 * requests + 2 * t + 1])
            for t in range(per)
        ],
        axis=0,
    )
    lane = lax.broadcasted_iota(jnp.int32, (rows, HD), 1)
    stats = jnp.zeros((rows, HD), jnp.float32)
    for h in range(heads):
        cols = slice(h * HD, (h + 1) * HD)
        scores = []
        for t in range(per):
            keys = jnp.concatenate([pick(k_here, k_side, 2 * t + j, cols) for j in range(2)], axis=0)
            scores.append(
                lax.dot_general(
                    q_ref[t * STRETCH : (t + 1) * STRETCH, cols],
                    keys,
                    (((1,), (1,)), ((), ())),
                    preferred_element_type=jnp.float32,
                )
            )
        scores = jnp.where(have > 0, jnp.concatenate(scores, axis=0), HIDDEN)
        top = jnp.maximum(jnp.max(scores, axis=1, keepdims=True), FLOOR)
        weights = jnp.exp2((scores - top) * EXP_SCALE)
        total = jnp.sum(weights, axis=1, keepdims=True)
        weights = weights.astype(jnp.bfloat16)
        stats = jnp.where(lane == h, top, jnp.where(lane == heads + h, total, stats))
        for t in range(per):
            values = jnp.concatenate([pick(v_here, v_side, 2 * t + j, cols) for j in range(2)], axis=0)
            o_ref[t * STRETCH : (t + 1) * STRETCH, cols] = jnp.dot(
                weights[t * STRETCH : (t + 1) * STRETCH],
                values,
                preferred_element_type=jnp.float32,
            ).astype(o_ref.dtype)
    column[...] = stats
    stats = jnp.transpose(column[...])[: 2 * heads, :]
    if travels:
        for i in range(3):
            piece = stats.astype(jnp.bfloat16)
            o_ref[rows : rows + 2 * heads, i * rows : (i + 1) * rows] = piece
            stats = stats - piece.astype(jnp.float32)
        o_ref[rows : rows + 2 * heads, 3 * rows :] = jnp.zeros(
            (2 * heads, width - 3 * rows), jnp.bfloat16
        )
    else:
        stat_ref[...] = stats


def cross_part(meta, queries, pool, travels, after, cost):
    rows, width = queries.shape
    heads = width // HD
    vmem = pl.BlockSpec(memory_space=pltpu.VMEM)
    if travels:
        out_specs = vmem
        out_shape = jax.ShapeDtypeStruct((rows + 2 * heads, width), jnp.bfloat16)
    else:
        out_specs = (vmem, vmem)
        out_shape = (
            jax.ShapeDtypeStruct((rows, width), jnp.float32),
            jax.ShapeDtypeStruct((2 * heads, rows), jnp.float32),
        )
    return pl.pallas_call(
        functools.partial(cross_kernel, rows // STRETCH, travels),
        in_specs=[pl.BlockSpec(memory_space=pltpu.SMEM)]
        + [vmem] * 4
        + [pl.BlockSpec(memory_space=pl.ANY)] * len(after),
        out_specs=out_specs,
        out_shape=out_shape,
        scratch_shapes=[pltpu.VMEM((rows, HD), jnp.float32)],
        compiler_params=pltpu.CompilerParams(vmem_limit_bytes=32 * 1024 * 1024),
        cost_estimate=cost,
    )(meta, queries, *pool, *after)


def merge_kernel(oa_ref, ob_ref, sa_ref, out_ref):
    rows, width = oa_ref.shape
    heads = width // HD
    pieces = ob_ref[rows : rows + 2 * heads, : 3 * rows].astype(jnp.float32)
    far = pieces[:, :rows] + pieces[:, rows : 2 * rows] + pieces[:, 2 * rows :]
    fill = jnp.zeros((HD - 4 * heads, rows), jnp.float32)
    stats = jnp.transpose(jnp.concatenate([sa_ref[...], far, fill], axis=0))
    for h in range(heads):
        cols = slice(h * HD, (h + 1) * HD)
        top_a, total_a, top_b, total_b = (
            stats[:, i * heads + h : i * heads + h + 1] for i in range(4)
        )
        top = jnp.maximum(top_a, top_b)
        part_a = jnp.exp2((top_a - top) * EXP_SCALE)
        part_b = jnp.exp2((top_b - top) * EXP_SCALE)
        share = 1.0 / (total_a * part_a + total_b * part_b)
        out_ref[:, cols] = (
            oa_ref[:, cols] * (part_a * share)
            + ob_ref[:rows, cols].astype(jnp.float32) * (part_b * share)
        ).astype(out_ref.dtype)


def merge(oa, ob, sa):
    rows, width = oa.shape
    vmem = pl.BlockSpec(memory_space=pltpu.VMEM)
    return pl.pallas_call(
        merge_kernel,
        in_specs=[vmem] * 3,
        out_specs=vmem,
        out_shape=jax.ShapeDtypeStruct((rows, width), jnp.bfloat16),
        compiler_params=pltpu.CompilerParams(vmem_limit_bytes=32 * 1024 * 1024),
        cost_estimate=SMALL,
    )(oa, ob, sa)


def shards(
    self_queries,
    self_keys,
    self_values,
    cross_queries,
    neighbour_keys,
    neighbour_values,
    neighbour_table,
    doc_lengths,
):
    tokens, width = self_queries.shape
    part = width // 2
    device = lax.axis_index(ALL)
    core = device % 2
    zhi = (device // 2) % 2
    chip = device // 2

    far_queries = swap(cross_queries, 2)

    which = core.astype(jnp.int32).reshape(1)
    trio = (self_keys, self_values, self_queries)
    beside = swap(cut(which, trio), 1)
    kv0, q0 = join(which, trio, beside)
    pool = held_back(jnp.stack([neighbour_keys, neighbour_values]), (kv0,))
    pool_beside = swap(pool, 1)

    base = jnp.stack([chip * 2 * tokens + core * tokens, chip * 2 * tokens + (1 - core) * tokens])
    positions = (base[:, None] + jnp.arange(tokens, dtype=jnp.int32)[None, :]).reshape(-1)
    ends = jnp.cumsum(doc_lengths)
    starts = jnp.sum(jnp.where(ends[None, :] <= positions[:, None], doc_lengths[None, :], 0), axis=1)
    low, high = place(device)
    flags = [
        low > 0,
        (low == 0) & (high == 1),
        (low == 0) & (high == 0),
        low < RUN - 1,
        low == RUN - 1,
    ]
    self_meta = jnp.stack(
        [base[0], base[1], jnp.minimum(starts[0], starts[tokens]), *flags], dtype=jnp.int32
    )
    starts_wide = jnp.broadcast_to(starts[:, None], (2 * tokens, HD)).astype(jnp.int32)

    def attend(blocks, pairs, state, last=False, after=(), cost=SMALL):
        return self_part(
            self_meta, q0, starts_wide, blocks, pairs, state, last, after, cost
        )

    kv3 = shift(kv0, 6)
    kv2 = shift(kv0, 4)
    kv4_far = shift(kv0, 8, lambda low, high: low == 0 and high == 1)

    state = attend(((0, 0),), (kv0,), None, cost=LARGE)
    def pool_meta(owner):
        per = tokens // STRETCH
        ids = lax.dynamic_slice_in_dim(neighbour_table, owner * per, per, 0).reshape(-1)
        holder, slot = ids // neighbour_keys.shape[0], ids % neighbour_keys.shape[0]
        return jnp.concatenate([slot, holder % 2 != core, holder // 2 == zhi]).astype(jnp.int32)

    pool = (neighbour_keys, neighbour_values, pool_beside)
    near_sum, near_stat = cross_part(
        pool_meta(device), cross_queries, pool, False, state[:1], SMALL
    )
    far_sum = cross_part(
        pool_meta(device ^ 2), far_queries, pool, True, (near_stat,), SMALL
    )
    nearly = around(far_sum, 7)
    from_first = jnp.where(high == 0, kv2, kv4_far)
    state = attend(((2, 0),), (kv2,), state, after=(far_sum, from_first))
    kv2 = held_back(kv2, state[:1])
    kv4 = shift(kv2, 4, lambda low, high: low > 0)
    kv1_edge = lax.ppermute(
        from_first,
        ALL,
        [
            (d, (d - 2 - 4 * place(d)[1]) % lax.axis_size(ALL))
            for d in range(lax.axis_size(ALL))
            if place(d)[0] == 0
        ],
    )
    kv3 = held_back(kv3, (kv2, nearly))
    kv1 = shift(kv3, -4, lambda low, high: low < RUN - 1)
    kv4_last = shift(kv3, 2, lambda low, high: low == 0 and high == 0)
    back_sum = around(nearly, 1)
    state = attend(((4, 1), (4, 2), (3, 0)), (kv4, kv4_far, kv3), state)
    kept, sent = attend(((4, 3), (1, 4), (1, 5)), (kv4_last, kv1, kv1_edge), state, True)
    returned = swap(sent, 1)
    self_out = jnp.where(
        core == 0,
        jnp.concatenate([kept, returned], axis=1),
        jnp.concatenate([returned, kept], axis=1),
    )
    cross_out = merge(near_sum, back_sum, near_stat)
    return self_out, cross_out


def solution(mesh):
    rows = P(("ctx", "nbr"), "mp")
    pool = P(("ctx", "nbr"), None, "mp")
    return jax.shard_map(
        shards,
        mesh=mesh,
        in_specs=(rows, rows, rows, rows, pool, pool, P(), P()),
        out_specs=(rows, rows),
        check_vma=False,
    )
```

```python
import functools
import jax
import jax.numpy as jnp
from jax import lax
from jax.experimental import pallas as pl
from jax.experimental.pallas import tpu as pltpu
from jax.sharding import PartitionSpec as P

HD = 128
STRETCH = 64
LOG2E = 1.4426950408889634
EXP_SCALE = LOG2E * HD**-0.5
HIDDEN = -1e30
FLOOR = -1e29
ALL = ("ctx", "nbr")
RUN = 8
SMALL = pl.CostEstimate(flops=1, bytes_accessed=1, transcendentals=0)
LARGE = pl.CostEstimate(flops=10**11, bytes_accessed=10**8, transcendentals=0)


def place(d):
    return d // 4 % RUN, d // 2 % 2


def shift(value, by, to=lambda low, high: True):
    count = lax.axis_size(ALL)
    pairs = [(d, (d + by) % count) for d in range(count)]
    return lax.ppermute(value, ALL, [(a, b) for a, b in pairs if to(*place(b))])


def swap(value, bit):
    count = lax.axis_size(ALL)
    return lax.ppermute(value, ALL, [(d, d ^ bit) for d in range(count)])


def around(value, by):
    count = lax.axis_size(ALL)

    def target(d):
        low, high = place(d)
        z = (high * RUN + low + by) % (2 * RUN)
        return d + (z % RUN - low) * 4 + (z // RUN - high) * 2

    return lax.ppermute(value, ALL, [(d, target(d)) for d in range(count)])


def held_back(value, after):
    hbm = pl.BlockSpec(memory_space=pl.ANY)
    return pl.pallas_call(
        lambda *refs: None,
        in_specs=[hbm] * (1 + len(after)),
        out_specs=hbm,
        out_shape=jax.ShapeDtypeStruct(value.shape, value.dtype),
        input_output_aliases={0: 0},
        cost_estimate=SMALL,
    )(value, *after)


def cut_kernel(core, a_ref, b_ref, c_ref, out_ref):
    out_ref[0] = a_ref[...]
    out_ref[1] = b_ref[...]
    out_ref[2] = c_ref[...]


def cut(core, arrays):
    rows, width = arrays[0].shape
    part = width // 2
    return pl.pallas_call(
        cut_kernel,
        grid_spec=pltpu.PrefetchScalarGridSpec(
            num_scalar_prefetch=1,
            grid=(1,),
            in_specs=[pl.BlockSpec((rows, part), lambda i, c: (0, 1 - c[0]))] * 3,
            out_specs=pl.BlockSpec((3, rows, part), lambda i, c: (0, 0, 0)),
        ),
        out_shape=jax.ShapeDtypeStruct((3, rows, part), arrays[0].dtype),
        cost_estimate=SMALL,
    )(core, *arrays)


def join_kernel(core, a_ref, b_ref, c_ref, beside_ref, pair_ref, single_ref):
    rows = a_ref.shape[0]
    for i, ref in enumerate((a_ref, b_ref)):
        pair_ref[i, :rows] = ref[...]
        pair_ref[i, rows:] = beside_ref[i]
    single_ref[:rows] = c_ref[...]
    single_ref[rows:] = beside_ref[2]


def join(core, arrays, beside):
    rows, width = arrays[0].shape
    part = width // 2
    dtype = arrays[0].dtype
    return pl.pallas_call(
        join_kernel,
        grid_spec=pltpu.PrefetchScalarGridSpec(
            num_scalar_prefetch=1,
            grid=(1,),
            in_specs=[pl.BlockSpec((rows, part), lambda i, c: (0, c[0]))] * 3
            + [pl.BlockSpec((3, rows, part), lambda i, c: (0, 0, 0))],
            out_specs=(
                pl.BlockSpec((2, 2 * rows, part), lambda i, c: (0, 0, 0)),
                pl.BlockSpec((2 * rows, part), lambda i, c: (0, 0)),
            ),
        ),
        out_shape=(
            jax.ShapeDtypeStruct((2, 2 * rows, part), dtype),
            jax.ShapeDtypeStruct((2 * rows, part), dtype),
        ),
        compiler_params=pltpu.CompilerParams(vmem_limit_bytes=32 * 1024 * 1024),
        cost_estimate=SMALL,
    )(core, *arrays, beside)


def self_kernel(blocks, first, last, skip, meta, *refs):
    refs = list(refs)
    q_ref = refs.pop(0)
    start_ref = refs.pop(0)
    pairs = [refs.pop(0) for _ in blocks]
    if not first:
        acc_in, top_in, total_in = refs.pop(0), refs.pop(0), refs.pop(0)
    refs = refs[skip:]
    if last:
        kept_ref, sent_ref = refs.pop(0), refs.pop(0)
    acc, top, total = refs
    rows = q_ref.shape[0]
    half = rows // 2
    if first:
        acc[...] = jnp.zeros_like(acc)
        top[...] = jnp.full_like(top, FLOOR)
        total[...] = jnp.zeros_like(total)
    else:
        acc[...] = acc_in[...]
        top[...] = top_in[...]
        total[...] = total_in[...]
    for bi, (back, flag) in enumerate(blocks):
        away = back * rows
        chip_first = jnp.minimum(meta[0], meta[1])
        seen = (chip_first - away + rows - 1 >= meta[2]) & (chip_first >= away)
        if flag:
            seen &= meta[2 + flag] > 0
        @pl.when(seen)
        def _(bi=bi, away=away):
            for qi in range(2):
                mine = pl.ds(qi * half, half)
                scores = lax.dot_general(
                    q_ref[mine, :],
                    pairs[bi][0],
                    (((1,), (1,)), ((), ())),
                    preferred_element_type=jnp.float32,
                )
                spot = lax.broadcasted_iota(jnp.int32, (half, half), 1)
                k_pos = jnp.concatenate([spot + meta[0], spot + meta[1]], axis=1) - away
                q_pos = meta[qi] + lax.broadcasted_iota(jnp.int32, (half, rows), 0)
                begin = jnp.concatenate([start_ref[mine, :]] * (rows // HD), axis=1)
                scores = jnp.where((k_pos <= q_pos) & (k_pos >= begin), scores, HIDDEN)
                old = top[0, mine, :]
                new = jnp.maximum(old, jnp.max(scores, axis=1, keepdims=True))
                wide = jnp.concatenate([new] * (rows // HD), axis=1)
                weights = jnp.exp2((scores - wide) * EXP_SCALE)
                factor = jnp.exp2((old - new) * EXP_SCALE)
                top[0, mine, :] = new
                total[0, mine, :] = total[0, mine, :] * factor + jnp.sum(
                    weights, axis=1, keepdims=True
                )
                acc[mine, :] = acc[mine, :] * factor + jnp.dot(
                    weights.astype(jnp.bfloat16), pairs[bi][1], preferred_element_type=jnp.float32
                )

    if last:
        out = (acc[...] / total[0]).astype(kept_ref.dtype)
        kept_ref[...] = out[:half]
        sent_ref[...] = out[half:]


def self_part(meta, queries, starts, blocks, pairs, state, last, after, cost):
    rows, width = queries.shape
    heads = width // HD
    column = pl.BlockSpec((rows, HD), lambda h: (0, h))
    pair = pl.BlockSpec((2, rows, HD), lambda h: (0, 0, h))
    stat = pl.BlockSpec((1, rows, HD), lambda h: (h, 0, 0))
    first = state is None
    in_specs = [
        pl.BlockSpec(memory_space=pltpu.SMEM),
        column,
        pl.BlockSpec((rows, HD), lambda h: (0, 0)),
    ] + [pair] * len(blocks)
    args = [meta, queries, starts, *pairs]
    if not first:
        in_specs += [column, stat, stat]
        args += list(state)
    in_specs += [pl.BlockSpec(memory_space=pl.ANY)] * len(after)
    args += list(after)
    if last:
        out_shape = (jax.ShapeDtypeStruct((rows // 2, width), jnp.bfloat16),) * 2
        out_specs = (pl.BlockSpec((rows // 2, HD), lambda h: (0, h)),) * 2
        scratch = [
            pltpu.VMEM((rows, HD), jnp.float32),
            pltpu.VMEM((1, rows, HD), jnp.float32),
            pltpu.VMEM((1, rows, HD), jnp.float32),
        ]
    else:
        out_shape = (
            jax.ShapeDtypeStruct((rows, width), jnp.float32),
            jax.ShapeDtypeStruct((heads, rows, HD), jnp.float32),
            jax.ShapeDtypeStruct((heads, rows, HD), jnp.float32),
        )
        out_specs = (column, stat, stat)
        scratch = []
    return pl.pallas_call(
        functools.partial(self_kernel, tuple(blocks), first, last, len(after)),
        grid=(heads,),
        in_specs=in_specs,
        out_specs=out_specs,
        out_shape=out_shape,
        scratch_shapes=scratch,
        compiler_params=pltpu.CompilerParams(vmem_limit_bytes=32 * 1024 * 1024),
        cost_estimate=cost,
    )(*args)


def cross_kernel(per, travels, meta, q_ref, k_here, v_here, side, *refs):
    if travels:
        o_ref, column = refs[-2:]
    else:
        o_ref, stat_ref, column = refs[-3:]
    k_side, v_side = side.at[0], side.at[1]
    length = k_here.shape[1]
    rows, width = q_ref.shape
    heads = width // HD
    requests = 2 * per

    def pick(here, side, r, cols):
        slot, beside = meta[r], meta[requests + r]
        return jnp.where(beside > 0, side[slot, :, cols], here[slot, :, cols])

    shape = (STRETCH, 2 * length)
    first = lax.broadcasted_iota(jnp.int32, shape, 1) < length
    have = jnp.concatenate(
        [
            jnp.where(first, meta[2 * requests + 2 * t], meta[2 * requests + 2 * t + 1])
            for t in range(per)
        ],
        axis=0,
    )
    lane = lax.broadcasted_iota(jnp.int32, (rows, HD), 1)
    stats = jnp.zeros((rows, HD), jnp.float32)
    for h in range(heads):
        cols = slice(h * HD, (h + 1) * HD)
        scores = []
        for t in range(per):
            keys = jnp.concatenate([pick(k_here, k_side, 2 * t + j, cols) for j in range(2)], axis=0)
            scores.append(
                lax.dot_general(
                    q_ref[t * STRETCH : (t + 1) * STRETCH, cols],
                    keys,
                    (((1,), (1,)), ((), ())),
                    preferred_element_type=jnp.float32,
                )
            )
        scores = jnp.where(have > 0, jnp.concatenate(scores, axis=0), HIDDEN)
        top = jnp.maximum(jnp.max(scores, axis=1, keepdims=True), FLOOR)
        weights = jnp.exp2((scores - top) * EXP_SCALE)
        total = jnp.sum(weights, axis=1, keepdims=True)
        weights = weights.astype(jnp.bfloat16)
        stats = jnp.where(lane == h, top, jnp.where(lane == heads + h, total, stats))
        for t in range(per):
            values = jnp.concatenate([pick(v_here, v_side, 2 * t + j, cols) for j in range(2)], axis=0)
            o_ref[t * STRETCH : (t + 1) * STRETCH, cols] = jnp.dot(
                weights[t * STRETCH : (t + 1) * STRETCH],
                values,
                preferred_element_type=jnp.float32,
            ).astype(o_ref.dtype)
    column[...] = stats
    stats = jnp.transpose(column[...])[: 2 * heads, :]
    if travels:
        for i in range(3):
            piece = stats.astype(jnp.bfloat16)
            o_ref[rows : rows + 2 * heads, i * rows : (i + 1) * rows] = piece
            stats = stats - piece.astype(jnp.float32)
        o_ref[rows : rows + 2 * heads, 3 * rows :] = jnp.zeros(
            (2 * heads, width - 3 * rows), jnp.bfloat16
        )
    else:
        stat_ref[...] = stats


def cross_part(meta, queries, pool, travels, after, cost):
    rows, width = queries.shape
    heads = width // HD
    vmem = pl.BlockSpec(memory_space=pltpu.VMEM)
    if travels:
        out_specs = vmem
        out_shape = jax.ShapeDtypeStruct((rows + 2 * heads, width), jnp.bfloat16)
    else:
        out_specs = (vmem, vmem)
        out_shape = (
            jax.ShapeDtypeStruct((rows, width), jnp.float32),
            jax.ShapeDtypeStruct((2 * heads, rows), jnp.float32),
        )
    return pl.pallas_call(
        functools.partial(cross_kernel, rows // STRETCH, travels),
        in_specs=[pl.BlockSpec(memory_space=pltpu.SMEM)]
        + [vmem] * 4
        + [pl.BlockSpec(memory_space=pl.ANY)] * len(after),
        out_specs=out_specs,
        out_shape=out_shape,
        scratch_shapes=[pltpu.VMEM((rows, HD), jnp.float32)],
        compiler_params=pltpu.CompilerParams(vmem_limit_bytes=32 * 1024 * 1024),
        cost_estimate=cost,
    )(meta, queries, *pool, *after)


def merge_kernel(oa_ref, ob_ref, sa_ref, out_ref):
    rows, width = oa_ref.shape
    heads = width // HD
    pieces = ob_ref[rows : rows + 2 * heads, : 3 * rows].astype(jnp.float32)
    far = pieces[:, :rows] + pieces[:, rows : 2 * rows] + pieces[:, 2 * rows :]
    fill = jnp.zeros((HD - 4 * heads, rows), jnp.float32)
    stats = jnp.transpose(jnp.concatenate([sa_ref[...], far, fill], axis=0))
    for h in range(heads):
        cols = slice(h * HD, (h + 1) * HD)
        top_a, total_a, top_b, total_b = (
            stats[:, i * heads + h : i * heads + h + 1] for i in range(4)
        )
        top = jnp.maximum(top_a, top_b)
        part_a = jnp.exp2((top_a - top) * EXP_SCALE)
        part_b = jnp.exp2((top_b - top) * EXP_SCALE)
        share = 1.0 / (total_a * part_a + total_b * part_b)
        out_ref[:, cols] = (
            oa_ref[:, cols] * (part_a * share)
            + ob_ref[:rows, cols].astype(jnp.float32) * (part_b * share)
        ).astype(out_ref.dtype)


def merge(oa, ob, sa):
    rows, width = oa.shape
    vmem = pl.BlockSpec(memory_space=pltpu.VMEM)
    return pl.pallas_call(
        merge_kernel,
        in_specs=[vmem] * 3,
        out_specs=vmem,
        out_shape=jax.ShapeDtypeStruct((rows, width), jnp.bfloat16),
        compiler_params=pltpu.CompilerParams(vmem_limit_bytes=32 * 1024 * 1024),
        cost_estimate=SMALL,
    )(oa, ob, sa)


def shards(
    self_queries,
    self_keys,
    self_values,
    cross_queries,
    neighbour_keys,
    neighbour_values,
    neighbour_table,
    doc_lengths,
):
    tokens, width = self_queries.shape
    part = width // 2
    device = lax.axis_index(ALL)
    core = device % 2
    zhi = (device // 2) % 2
    chip = device // 2

    far_queries = swap(cross_queries, 2)

    which = core.astype(jnp.int32).reshape(1)
    trio = (self_keys, self_values, self_queries)
    beside = swap(cut(which, trio), 1)
    kv0, q0 = join(which, trio, beside)
    pool = held_back(jnp.stack([neighbour_keys, neighbour_values]), (kv0,))
    pool_beside = swap(pool, 1)

    base = jnp.stack([chip * 2 * tokens + core * tokens, chip * 2 * tokens + (1 - core) * tokens])
    positions = (base[:, None] + jnp.arange(tokens, dtype=jnp.int32)[None, :]).reshape(-1)
    ends = jnp.cumsum(doc_lengths)
    starts = jnp.sum(jnp.where(ends[None, :] <= positions[:, None], doc_lengths[None, :], 0), axis=1)
    low, high = place(device)
    flags = [
        low > 0,
        (low == 0) & (high == 1),
        (low == 0) & (high == 0),
        low < RUN - 1,
        low == RUN - 1,
    ]
    self_meta = jnp.stack(
        [base[0], base[1], jnp.minimum(starts[0], starts[tokens]), *flags], dtype=jnp.int32
    )
    starts_wide = jnp.broadcast_to(starts[:, None], (2 * tokens, HD)).astype(jnp.int32)

    def attend(blocks, pairs, state, last=False, after=(), cost=SMALL):
        return self_part(
            self_meta, q0, starts_wide, blocks, pairs, state, last, after, cost
        )

    kv3 = shift(kv0, 6)
    kv2 = shift(kv0, 4)
    kv4_far = shift(kv0, 8, lambda low, high: low == 0 and high == 1)

    state = attend(((0, 0),), (kv0,), None, cost=LARGE)
    def pool_meta(owner):
        per = tokens // STRETCH
        ids = lax.dynamic_slice_in_dim(neighbour_table, owner * per, per, 0).reshape(-1)
        holder, slot = ids // neighbour_keys.shape[0], ids % neighbour_keys.shape[0]
        return jnp.concatenate([slot, holder % 2 != core, holder // 2 == zhi]).astype(jnp.int32)

    pool = (neighbour_keys, neighbour_values, pool_beside)
    near_sum, near_stat = cross_part(
        pool_meta(device), cross_queries, pool, False, state[:1], SMALL
    )
    far_sum = cross_part(
        pool_meta(device ^ 2), far_queries, pool, True, (near_stat,), SMALL
    )
    nearly = around(far_sum, 7)
    kv2 = held_back(kv2, (nearly,))
    kv4 = shift(kv2, 4, lambda low, high: low > 0)
    kv1_edge = lax.ppermute(
        jnp.where(high == 0, kv2, kv4_far),
        ALL,
        [
            (d, (d - 2 - 4 * place(d)[1]) % lax.axis_size(ALL))
            for d in range(lax.axis_size(ALL))
            if place(d)[0] == 0
        ],
    )
    state = attend(((2, 0),), (kv2,), state)
    kv3 = held_back(kv3, (kv2, state[0]))
    kv1 = shift(kv3, -4, lambda low, high: low < RUN - 1)
    kv4_last = shift(kv3, 2, lambda low, high: low == 0 and high == 0)
    back_sum = around(nearly, 1)
    state = attend(((4, 1), (4, 2), (3, 0)), (kv4, kv4_far, kv3), state)
    kept, sent = attend(((4, 3), (1, 4), (1, 5)), (kv4_last, kv1, kv1_edge), state, True)
    returned = swap(sent, 1)
    self_out = jnp.where(
        core == 0,
        jnp.concatenate([kept, returned], axis=1),
        jnp.concatenate([returned, kept], axis=1),
    )
    cross_out = merge(near_sum, back_sum, near_stat)
    return self_out, cross_out


def solution(mesh):
    rows = P(("ctx", "nbr"), "mp")
    pool = P(("ctx", "nbr"), None, "mp")
    return jax.shard_map(
        shards,
        mesh=mesh,
        in_specs=(rows, rows, rows, rows, pool, pool, P(), P()),
        out_specs=(rows, rows),
        check_vma=False,
    )
```

```python
import functools
import jax
import jax.numpy as jnp
from jax import lax
from jax.experimental import pallas as pl
from jax.experimental.pallas import tpu as pltpu
from jax.sharding import PartitionSpec as P

HD = 128
STRETCH = 64
LOG2E = 1.4426950408889634
EXP_SCALE = LOG2E * HD**-0.5
HIDDEN = -1e30
FLOOR = -1e29
ALL = ("ctx", "nbr")
RUN = 8
SMALL = pl.CostEstimate(flops=1, bytes_accessed=1, transcendentals=0)
LARGE = pl.CostEstimate(flops=10**11, bytes_accessed=10**8, transcendentals=0)


def place(d):
    return d // 4 % RUN, d // 2 % 2


def shift(value, by, to=lambda low, high: True):
    count = lax.axis_size(ALL)
    pairs = [(d, (d + by) % count) for d in range(count)]
    return lax.ppermute(value, ALL, [(a, b) for a, b in pairs if to(*place(b))])


def swap(value, bit):
    count = lax.axis_size(ALL)
    return lax.ppermute(value, ALL, [(d, d ^ bit) for d in range(count)])


def around(value, by):
    count = lax.axis_size(ALL)

    def target(d):
        low, high = place(d)
        z = (high * RUN + low + by) % (2 * RUN)
        return d + (z % RUN - low) * 4 + (z // RUN - high) * 2

    return lax.ppermute(value, ALL, [(d, target(d)) for d in range(count)])


def held_back(value, after):
    hbm = pl.BlockSpec(memory_space=pl.ANY)
    return pl.pallas_call(
        lambda *refs: None,
        in_specs=[hbm] * (1 + len(after)),
        out_specs=hbm,
        out_shape=jax.ShapeDtypeStruct(value.shape, value.dtype),
        input_output_aliases={0: 0},
        cost_estimate=SMALL,
    )(value, *after)


def cut_kernel(core, a_ref, b_ref, c_ref, out_ref):
    out_ref[0] = a_ref[...]
    out_ref[1] = b_ref[...]
    out_ref[2] = c_ref[...]


def cut(core, arrays):
    rows, width = arrays[0].shape
    part = width // 2
    return pl.pallas_call(
        cut_kernel,
        grid_spec=pltpu.PrefetchScalarGridSpec(
            num_scalar_prefetch=1,
            grid=(1,),
            in_specs=[pl.BlockSpec((rows, part), lambda i, c: (0, 1 - c[0]))] * 3,
            out_specs=pl.BlockSpec((3, rows, part), lambda i, c: (0, 0, 0)),
        ),
        out_shape=jax.ShapeDtypeStruct((3, rows, part), arrays[0].dtype),
        cost_estimate=SMALL,
    )(core, *arrays)


def join_kernel(core, a_ref, b_ref, c_ref, beside_ref, pair_ref, single_ref):
    rows = a_ref.shape[0]
    for i, ref in enumerate((a_ref, b_ref)):
        pair_ref[i, :rows] = ref[...]
        pair_ref[i, rows:] = beside_ref[i]
    single_ref[:rows] = c_ref[...]
    single_ref[rows:] = beside_ref[2]


def join(core, arrays, beside):
    rows, width = arrays[0].shape
    part = width // 2
    dtype = arrays[0].dtype
    return pl.pallas_call(
        join_kernel,
        grid_spec=pltpu.PrefetchScalarGridSpec(
            num_scalar_prefetch=1,
            grid=(1,),
            in_specs=[pl.BlockSpec((rows, part), lambda i, c: (0, c[0]))] * 3
            + [pl.BlockSpec((3, rows, part), lambda i, c: (0, 0, 0))],
            out_specs=(
                pl.BlockSpec((2, 2 * rows, part), lambda i, c: (0, 0, 0)),
                pl.BlockSpec((2 * rows, part), lambda i, c: (0, 0)),
            ),
        ),
        out_shape=(
            jax.ShapeDtypeStruct((2, 2 * rows, part), dtype),
            jax.ShapeDtypeStruct((2 * rows, part), dtype),
        ),
        compiler_params=pltpu.CompilerParams(vmem_limit_bytes=32 * 1024 * 1024),
        cost_estimate=SMALL,
    )(core, *arrays, beside)


def self_kernel(blocks, first, last, skip, meta, *refs):
    refs = list(refs)
    q_ref = refs.pop(0)
    start_ref = refs.pop(0)
    pairs = [refs.pop(0) for _ in blocks]
    if not first:
        acc_in, top_in, total_in = refs.pop(0), refs.pop(0), refs.pop(0)
    refs = refs[skip:]
    if last:
        kept_ref, sent_ref = refs.pop(0), refs.pop(0)
    acc, top, total = refs
    rows = q_ref.shape[0]
    half = rows // 2
    if first:
        acc[...] = jnp.zeros_like(acc)
        top[...] = jnp.full_like(top, FLOOR)
        total[...] = jnp.zeros_like(total)
    else:
        acc[...] = acc_in[...]
        top[...] = top_in[...]
        total[...] = total_in[...]
    for bi, (back, flag) in enumerate(blocks):
        away = back * rows
        chip_first = jnp.minimum(meta[0], meta[1])
        seen = (chip_first - away + rows - 1 >= meta[2]) & (chip_first >= away)
        if flag:
            seen &= meta[2 + flag] > 0
        @pl.when(seen)
        def _(bi=bi, away=away):
            for qi in range(2):
                mine = pl.ds(qi * half, half)
                scores = lax.dot_general(
                    q_ref[mine, :],
                    pairs[bi][0],
                    (((1,), (1,)), ((), ())),
                    preferred_element_type=jnp.float32,
                )
                spot = lax.broadcasted_iota(jnp.int32, (half, half), 1)
                k_pos = jnp.concatenate([spot + meta[0], spot + meta[1]], axis=1) - away
                q_pos = meta[qi] + lax.broadcasted_iota(jnp.int32, (half, rows), 0)
                begin = jnp.concatenate([start_ref[mine, :]] * (rows // HD), axis=1)
                scores = jnp.where((k_pos <= q_pos) & (k_pos >= begin), scores, HIDDEN)
                old = top[0, mine, :]
                new = jnp.maximum(old, jnp.max(scores, axis=1, keepdims=True))
                wide = jnp.concatenate([new] * (rows // HD), axis=1)
                weights = jnp.exp2((scores - wide) * EXP_SCALE)
                factor = jnp.exp2((old - new) * EXP_SCALE)
                top[0, mine, :] = new
                total[0, mine, :] = total[0, mine, :] * factor + jnp.sum(
                    weights, axis=1, keepdims=True
                )
                acc[mine, :] = acc[mine, :] * factor + jnp.dot(
                    weights.astype(jnp.bfloat16), pairs[bi][1], preferred_element_type=jnp.float32
                )

    if last:
        out = (acc[...] / total[0]).astype(kept_ref.dtype)
        kept_ref[...] = out[:half]
        sent_ref[...] = out[half:]


def self_part(meta, queries, starts, blocks, pairs, state, last, after, cost):
    rows, width = queries.shape
    heads = width // HD
    column = pl.BlockSpec((rows, HD), lambda h: (0, h))
    pair = pl.BlockSpec((2, rows, HD), lambda h: (0, 0, h))
    stat = pl.BlockSpec((1, rows, HD), lambda h: (h, 0, 0))
    first = state is None
    in_specs = [
        pl.BlockSpec(memory_space=pltpu.SMEM),
        column,
        pl.BlockSpec((rows, HD), lambda h: (0, 0)),
    ] + [pair] * len(blocks)
    args = [meta, queries, starts, *pairs]
    if not first:
        in_specs += [column, stat, stat]
        args += list(state)
    in_specs += [pl.BlockSpec(memory_space=pl.ANY)] * len(after)
    args += list(after)
    if last:
        out_shape = (jax.ShapeDtypeStruct((rows // 2, width), jnp.bfloat16),) * 2
        out_specs = (pl.BlockSpec((rows // 2, HD), lambda h: (0, h)),) * 2
        scratch = [
            pltpu.VMEM((rows, HD), jnp.float32),
            pltpu.VMEM((1, rows, HD), jnp.float32),
            pltpu.VMEM((1, rows, HD), jnp.float32),
        ]
    else:
        out_shape = (
            jax.ShapeDtypeStruct((rows, width), jnp.float32),
            jax.ShapeDtypeStruct((heads, rows, HD), jnp.float32),
            jax.ShapeDtypeStruct((heads, rows, HD), jnp.float32),
        )
        out_specs = (column, stat, stat)
        scratch = []
    return pl.pallas_call(
        functools.partial(self_kernel, tuple(blocks), first, last, len(after)),
        grid=(heads,),
        in_specs=in_specs,
        out_specs=out_specs,
        out_shape=out_shape,
        scratch_shapes=scratch,
        compiler_params=pltpu.CompilerParams(vmem_limit_bytes=32 * 1024 * 1024),
        cost_estimate=cost,
    )(*args)


def cross_kernel(per, travels, meta, q_ref, k_here, v_here, side, *refs):
    if travels:
        o_ref, column = refs[-2:]
    else:
        o_ref, stat_ref, column = refs[-3:]
    k_side, v_side = side.at[0], side.at[1]
    length = k_here.shape[1]
    rows, width = q_ref.shape
    heads = width // HD
    requests = 2 * per

    def pick(here, side, r, cols):
        slot, beside = meta[r], meta[requests + r]
        return jnp.where(beside > 0, side[slot, :, cols], here[slot, :, cols])

    shape = (STRETCH, 2 * length)
    first = lax.broadcasted_iota(jnp.int32, shape, 1) < length
    have = jnp.concatenate(
        [
            jnp.where(first, meta[2 * requests + 2 * t], meta[2 * requests + 2 * t + 1])
            for t in range(per)
        ],
        axis=0,
    )
    lane = lax.broadcasted_iota(jnp.int32, (rows, HD), 1)
    stats = jnp.zeros((rows, HD), jnp.float32)
    for h in range(heads):
        cols = slice(h * HD, (h + 1) * HD)
        scores = []
        for t in range(per):
            keys = jnp.concatenate([pick(k_here, k_side, 2 * t + j, cols) for j in range(2)], axis=0)
            scores.append(
                lax.dot_general(
                    q_ref[t * STRETCH : (t + 1) * STRETCH, cols],
                    keys,
                    (((1,), (1,)), ((), ())),
                    preferred_element_type=jnp.float32,
                )
            )
        scores = jnp.where(have > 0, jnp.concatenate(scores, axis=0), HIDDEN)
        top = jnp.maximum(jnp.max(scores, axis=1, keepdims=True), FLOOR)
        weights = jnp.exp2((scores - top) * EXP_SCALE)
        total = jnp.sum(weights, axis=1, keepdims=True)
        weights = weights.astype(jnp.bfloat16)
        stats = jnp.where(lane == h, top, jnp.where(lane == heads + h, total, stats))
        for t in range(per):
            values = jnp.concatenate([pick(v_here, v_side, 2 * t + j, cols) for j in range(2)], axis=0)
            o_ref[t * STRETCH : (t + 1) * STRETCH, cols] = jnp.dot(
                weights[t * STRETCH : (t + 1) * STRETCH],
                values,
                preferred_element_type=jnp.float32,
            ).astype(o_ref.dtype)
    column[...] = stats
    stats = jnp.transpose(column[...])[: 2 * heads, :]
    if travels:
        for i in range(3):
            piece = stats.astype(jnp.bfloat16)
            o_ref[rows : rows + 2 * heads, i * rows : (i + 1) * rows] = piece
            stats = stats - piece.astype(jnp.float32)
        o_ref[rows : rows + 2 * heads, 3 * rows :] = jnp.zeros(
            (2 * heads, width - 3 * rows), jnp.bfloat16
        )
    else:
        stat_ref[...] = stats


def cross_part(meta, queries, pool, travels, after, cost):
    rows, width = queries.shape
    heads = width // HD
    vmem = pl.BlockSpec(memory_space=pltpu.VMEM)
    if travels:
        out_specs = vmem
        out_shape = jax.ShapeDtypeStruct((rows + 2 * heads, width), jnp.bfloat16)
    else:
        out_specs = (vmem, vmem)
        out_shape = (
            jax.ShapeDtypeStruct((rows, width), jnp.float32),
            jax.ShapeDtypeStruct((2 * heads, rows), jnp.float32),
        )
    return pl.pallas_call(
        functools.partial(cross_kernel, rows // STRETCH, travels),
        in_specs=[pl.BlockSpec(memory_space=pltpu.SMEM)]
        + [vmem] * 4
        + [pl.BlockSpec(memory_space=pl.ANY)] * len(after),
        out_specs=out_specs,
        out_shape=out_shape,
        scratch_shapes=[pltpu.VMEM((rows, HD), jnp.float32)],
        compiler_params=pltpu.CompilerParams(vmem_limit_bytes=32 * 1024 * 1024),
        cost_estimate=cost,
    )(meta, queries, *pool, *after)


def merge_kernel(oa_ref, ob_ref, sa_ref, out_ref):
    rows, width = oa_ref.shape
    heads = width // HD
    pieces = ob_ref[rows : rows + 2 * heads, : 3 * rows].astype(jnp.float32)
    far = pieces[:, :rows] + pieces[:, rows : 2 * rows] + pieces[:, 2 * rows :]
    fill = jnp.zeros((HD - 4 * heads, rows), jnp.float32)
    stats = jnp.transpose(jnp.concatenate([sa_ref[...], far, fill], axis=0))
    for h in range(heads):
        cols = slice(h * HD, (h + 1) * HD)
        top_a, total_a, top_b, total_b = (
            stats[:, i * heads + h : i * heads + h + 1] for i in range(4)
        )
        top = jnp.maximum(top_a, top_b)
        part_a = jnp.exp2((top_a - top) * EXP_SCALE)
        part_b = jnp.exp2((top_b - top) * EXP_SCALE)
        share = 1.0 / (total_a * part_a + total_b * part_b)
        out_ref[:, cols] = (
            oa_ref[:, cols] * (part_a * share)
            + ob_ref[:rows, cols].astype(jnp.float32) * (part_b * share)
        ).astype(out_ref.dtype)


def merge(oa, ob, sa):
    rows, width = oa.shape
    vmem = pl.BlockSpec(memory_space=pltpu.VMEM)
    return pl.pallas_call(
        merge_kernel,
        in_specs=[vmem] * 3,
        out_specs=vmem,
        out_shape=jax.ShapeDtypeStruct((rows, width), jnp.bfloat16),
        compiler_params=pltpu.CompilerParams(vmem_limit_bytes=32 * 1024 * 1024),
        cost_estimate=SMALL,
    )(oa, ob, sa)


def shards(
    self_queries,
    self_keys,
    self_values,
    cross_queries,
    neighbour_keys,
    neighbour_values,
    neighbour_table,
    doc_lengths,
):
    tokens, width = self_queries.shape
    part = width // 2
    device = lax.axis_index(ALL)
    core = device % 2
    zhi = (device // 2) % 2
    chip = device // 2

    far_queries = swap(cross_queries, 2)

    which = core.astype(jnp.int32).reshape(1)
    trio = (self_keys, self_values, self_queries)
    beside = swap(cut(which, trio), 1)
    kv0, q0 = join(which, trio, beside)
    pool = held_back(jnp.stack([neighbour_keys, neighbour_values]), (kv0,))
    pool_beside = swap(pool, 1)

    base = jnp.stack([chip * 2 * tokens + core * tokens, chip * 2 * tokens + (1 - core) * tokens])
    positions = (base[:, None] + jnp.arange(tokens, dtype=jnp.int32)[None, :]).reshape(-1)
    ends = jnp.cumsum(doc_lengths)
    starts = jnp.sum(jnp.where(ends[None, :] <= positions[:, None], doc_lengths[None, :], 0), axis=1)
    low, high = place(device)
    flags = [
        low > 0,
        (low == 0) & (high == 1),
        (low == 0) & (high == 0),
        low < RUN - 1,
        low == RUN - 1,
    ]
    self_meta = jnp.stack(
        [base[0], base[1], jnp.minimum(starts[0], starts[tokens]), *flags], dtype=jnp.int32
    )
    starts_wide = jnp.broadcast_to(starts[:, None], (2 * tokens, HD)).astype(jnp.int32)

    def attend(blocks, pairs, state, last=False, after=(), cost=SMALL):
        return self_part(
            self_meta, q0, starts_wide, blocks, pairs, state, last, after, cost
        )

    kv3 = shift(kv0, 6)
    kv2 = shift(kv0, 4)
    kv4_far = shift(kv0, 8, lambda low, high: low == 0 and high == 1)

    state = attend(((0, 0),), (kv0,), None, cost=LARGE)
    def pool_meta(owner):
        per = tokens // STRETCH
        ids = lax.dynamic_slice_in_dim(neighbour_table, owner * per, per, 0).reshape(-1)
        holder, slot = ids // neighbour_keys.shape[0], ids % neighbour_keys.shape[0]
        return jnp.concatenate([slot, holder % 2 != core, holder // 2 == zhi]).astype(jnp.int32)

    pool = (neighbour_keys, neighbour_values, pool_beside)
    near_sum, near_stat = cross_part(
        pool_meta(device), cross_queries, pool, False, state[:1], SMALL
    )
    far_sum = cross_part(
        pool_meta(device ^ 2), far_queries, pool, True, (near_stat,), SMALL
    )
    nearly = around(far_sum, 7)
    from_first = jnp.where(high == 0, kv2, kv4_far)
    state = attend(((2, 0),), (kv2,), state, after=(far_sum, from_first))
    nearly = held_back(nearly, state[:1])
    kv2 = held_back(kv2, (nearly,))
    kv4 = shift(kv2, 4, lambda low, high: low > 0)
    kv1_edge = lax.ppermute(
        from_first,
        ALL,
        [
            (d, (d - 2 - 4 * place(d)[1]) % lax.axis_size(ALL))
            for d in range(lax.axis_size(ALL))
            if place(d)[0] == 0
        ],
    )
    kv3 = held_back(kv3, (kv2,))
    kv1 = shift(kv3, -4, lambda low, high: low < RUN - 1)
    kv4_last = shift(kv3, 2, lambda low, high: low == 0 and high == 0)
    back_sum = around(nearly, 1)
    state = attend(((4, 1), (4, 2), (3, 0)), (kv4, kv4_far, kv3), state)
    kept, sent = attend(((4, 3), (1, 4), (1, 5)), (kv4_last, kv1, kv1_edge), state, True)
    returned = swap(sent, 1)
    self_out = jnp.where(
        core == 0,
        jnp.concatenate([kept, returned], axis=1),
        jnp.concatenate([returned, kept], axis=1),
    )
    cross_out = merge(near_sum, back_sum, near_stat)
    return self_out, cross_out


def solution(mesh):
    rows = P(("ctx", "nbr"), "mp")
    pool = P(("ctx", "nbr"), None, "mp")
    return jax.shard_map(
        shards,
        mesh=mesh,
        in_specs=(rows, rows, rows, rows, pool, pool, P(), P()),
        out_specs=(rows, rows),
        check_vma=False,
    )
```
